256 devices in a mesh: src: 16 (over y, z_hi, core), tgt: 16 (over z_lo, x).
Axes of the slice: x: 4, y: 4, z: 8 (z_hi: 2, z_lo: 4; z = z_hi * 4 + z_lo), core: 2. Of those that a mesh axis runs over, the one named last changes fastest.
Arguments:
- sources: bfloat16 [32768, 128], P(('src', 'tgt')), may hold values from -4 to 4
- targets: bfloat16 [32768, 128], P('tgt'), may hold values from -4 to 4
- src_logmass: float32 [32768], P('src'), may hold values from -4 to 4
- tgt_logmass: float32 [32768], P('tgt'), may hold values from -4 to 4
Outputs:
- mapped: float32 [32768, 128], P(('src', 'tgt'))
- src_dual: float32 [32768], P('src')
- tgt_dual: float32 [32768], P('tgt')
The draws below stay inside these ranges and needn't reach their ends.
All inputs are finite; a program needn't handle non-finite values.
Results may differ from the reference program's by a relative error of at most 0.0003.
Values may be sent and summed in bfloat16 or wider, within the bound.
A program may use at most 64 MiB of HBM per device.

```python
import jax
import jax.numpy as jnp
from jax import lax

D = 128
SRC_DEV = 2048
ITERS = 2
NS = 32768
NT = 32768


def draw_sources(key, part):
    key = jax.random.fold_in(key, 11)
    values = jnp.clip(jax.random.normal(key, (NS, D), jnp.float32), -4.0, 4.0)
    return values.astype(jnp.bfloat16)


def draw_targets(key, part):
    key = jax.random.fold_in(key, 23)
    values = jnp.clip(jax.random.normal(key, (NT, D), jnp.float32), -4.0, 4.0)
    return values.astype(jnp.bfloat16)


def shard_levels(stream_key, dims, pieces, smallest, top_value):
    def one(axis_at, blocks):
        steps = jax.random.uniform(jax.random.fold_in(jax.random.fold_in(stream_key, 6), axis_at), (blocks,), jnp.float32, smallest / len(pieces), top_value / len(pieces))
        return jnp.repeat(jnp.exp(steps), dims[axis_at] // blocks).reshape((-1,) + (1,) * (len(dims) - axis_at - 1))

    level = one(*pieces[0])
    for cut in pieces[1:]:
        level = level * one(*cut)
    return level


def centred(stream_key, extent, width, bound, shards=(), kind=jnp.bfloat16):
    drawn = jax.random.normal(stream_key, extent, jnp.float32) * width
    if len(shards) > 0:
        drawn = shard_levels(stream_key, extent, shards, -0.22, 0.18) * drawn
    return jnp.clip(drawn, min=-bound, max=bound).astype(kind)


def setup_inputs(seed: int = 0) -> dict:
    splits = jax.random.split(jax.random.key(seed), 5)
    sources = draw_sources(jax.random.fold_in(splits[4], 71), 0)
    targets = draw_targets(jax.random.fold_in(splits[4], 71), 0)
    src_logmass = centred(splits[2], (NS,), 1.0, 4.0, ((0, 16),), jnp.float32)
    tgt_logmass = centred(splits[3], (NT,), 1.0, 4.0, ((0, 16),), jnp.float32)
    return dict(sources=sources, targets=targets, src_logmass=src_logmass, tgt_logmass=tgt_logmass)


entropy_weight = 0.03125


def reference(sources, targets, src_logmass, tgt_logmass):
    block_rows = SRC_DEV if SRC_DEV < 512 else 512
    block_count = NS // block_rows
    src_norm = 0.5 * jnp.sum(jnp.square(sources.astype(jnp.float32)), axis=1) / D
    tgt_norm = 0.5 * jnp.sum(jnp.square(targets.astype(jnp.float32)), axis=1) / D
    tgt_float = targets.astype(jnp.float32)
    src_blocks = sources.reshape(block_count, block_rows, D)
    norm_blocks = src_norm.reshape(block_count, block_rows)

    def cost_tile(src_block, src_part):
        inner = lax.dot_general(src_block, targets, (((1,), (1,)), ((), ())), preferred_element_type=jnp.float32)
        return src_part[:, None] + tgt_norm[None, :] - inner / D

    tgt_dual = jnp.zeros((NT,), jnp.float32)
    src_dual = jnp.zeros((NS,), jnp.float32)
    for iteration in range(ITERS):
        def row_lse(inputs, tgt_dual=tgt_dual):
            src_block, src_part = inputs
            scores = (tgt_dual[None, :] - cost_tile(src_block, src_part)) / entropy_weight
            highest = jnp.max(scores, axis=1)
            return highest + jnp.log(jnp.sum(jnp.exp(scores - highest[:, None]), axis=1))

        lse_rows = lax.map(row_lse, (src_blocks, norm_blocks)).reshape(NS)
        src_dual = entropy_weight * (src_logmass - lse_rows)
        dual_blocks = src_dual.reshape(block_count, block_rows)

        def col_step(carried, inputs):
            highest, summed = carried
            src_block, src_part, dual_part = inputs
            scores = (dual_part[:, None] - cost_tile(src_block, src_part)) / entropy_weight
            new_high = jnp.maximum(highest, jnp.max(scores, axis=0))
            summed = summed * jnp.exp(highest - new_high) + jnp.sum(jnp.exp(scores - new_high[None, :]), axis=0)
            return (new_high, summed), None

        starting = (jnp.full((NT,), -jnp.inf, jnp.float32), jnp.zeros((NT,), jnp.float32))
        (highest, summed), unused = lax.scan(col_step, starting, (src_blocks, norm_blocks, dual_blocks))
        tgt_dual = entropy_weight * (tgt_logmass - (highest + jnp.log(summed)))

    def map_block(inputs):
        src_block, src_part = inputs
        scores = (tgt_dual[None, :] - cost_tile(src_block, src_part)) / entropy_weight
        highest = jnp.max(scores, axis=1)
        weights = jnp.exp(scores - highest[:, None])
        row_mass = jnp.sum(weights, axis=1)
        row_moment = jnp.dot(weights, tgt_float, precision=lax.Precision.HIGHEST, preferred_element_type=jnp.float32)
        return row_moment / row_mass[:, None]

    mapped = lax.map(map_block, (src_blocks, norm_blocks)).reshape(NS, D)
    return mapped, src_dual, tgt_dual
```

```python
import functools
import math

import jax
import jax.numpy as jnp
from jax import lax
from jax.experimental import pallas as pl
from jax.experimental.pallas import tpu as pltpu
from jax.sharding import PartitionSpec as P

MESH = pl.DeviceIdType.MESH
EPS = 0.03125
LOG2E = math.log2(math.e)
B = 128
NB = 16
N = B * NB
D = 128
Q = 4
SCALE = LOG2E / (D * EPS)
BF = jnp.bfloat16
F32 = jnp.float32


def lse_sub(y):
    high = jnp.max(y, axis=0, keepdims=True)
    return high + jnp.log2(jnp.sum(jnp.exp2(y - high), axis=0, keepdims=True))


def tile_high(u):
    m = u[:, :B]
    for k in range(1, NB):
        m = jnp.maximum(m, u[:, k * B : (k + 1) * B])
    return m


def lse_block(lhs, rhs):
    u = jnp.dot(lhs, rhs, preferred_element_type=F32)
    m = tile_high(u)
    s = jnp.exp2((u[:, :B] - m) * SCALE)
    for k in range(1, NB):
        s = s + jnp.exp2((u[:, k * B : (k + 1) * B] - m) * SCALE)
    return lse_sub((m * SCALE + jnp.log2(s)).T)


def kernel(
    src_ref, tgt_ref, slm_ref, tlm_ref, map_ref, sd_ref, td_ref,
    codes, src_t, tgt_t, tgt_one, src_norm, tgt_norm, vec, lo_buf, hi_buf,
    part, got, part2, got2,
    g_hi_send, g_hi_recv, g_lo_send, g_lo_recv,
    e_send, e_recv, m_send, m_recv, r_send, r_recv,
):
    src_me = lax.axis_index("src")
    tgt_me = lax.axis_index("tgt")
    s_hi, s_lo = src_me // Q, src_me % Q
    t_hi, t_lo = tgt_me // Q, tgt_me % Q

    def lo_peer(axis, k):
        hi, lo = (s_hi, s_lo) if axis == "src" else (t_hi, t_lo)
        return {axis: hi * Q + (lo + k) % Q}

    def hi_peer(axis, k):
        hi, lo = (s_hi, s_lo) if axis == "src" else (t_hi, t_lo)
        return {axis: ((hi + k) % Q) * Q + lo}

    barrier = pltpu.get_barrier_semaphore()
    for axis in ("tgt", "src"):
        for k in range(1, Q):
            pl.semaphore_signal(barrier, 1, device_id=lo_peer(axis, k), device_id_type=MESH)
            pl.semaphore_signal(barrier, 1, device_id=hi_peer(axis, k), device_id_type=MESH)

    def copy(src, dst, send, recv, peer):
        return pltpu.make_async_remote_copy(
            src_ref=src, dst_ref=dst, send_sem=send, recv_sem=recv, device_id=peer, device_id_type=MESH
        )

    codes[tgt_me] = src_ref[...]
    pl.semaphore_wait(barrier, 4 * (Q - 1))

    def gather_hi(k):
        return copy(src_ref, codes.at[tgt_me], g_hi_send.at[k - 1], g_hi_recv.at[k - 1], hi_peer("tgt", k))

    def gather_lo(d, k):
        block = ((t_hi - d + Q) % Q) * Q + t_lo
        src = src_ref if isinstance(d, int) and d == 0 else codes.at[block]
        return copy(src, codes.at[block], g_lo_send.at[d, k - 1], g_lo_recv.at[d, k - 1], lo_peer("tgt", k))

    for k in range(1, Q):
        gather_hi(k).start()
    for k in range(1, Q):
        gather_lo(0, k).start()

    lane = lax.broadcasted_iota(jnp.int32, (B, D), 1)
    ones = jnp.where(lane < 3, 1.0, 0.0).astype(BF)
    sub16 = lax.broadcasted_iota(jnp.int32, (16, B), 0)

    src_t[pl.ds(D, D), :] = jnp.zeros((D, N), BF)
    tgt_t[pl.ds(D, D), :] = jnp.zeros((D, N), BF)
    tgt_one[:, pl.ds(D, D)] = jnp.ones((N, D), BF)

    def put_bias(rows_t, bias):
        hi = bias.astype(BF).astype(F32)
        rest = bias - hi
        mid = rest.astype(BF).astype(F32)
        low = rest - mid
        for k in range(NB):
            block = jnp.where(
                sub16 == 0, hi[k : k + 1, :],
                jnp.where(sub16 == 1, mid[k : k + 1, :], jnp.where(sub16 == 2, low[k : k + 1, :], 0.0)),
            )
            rows_t[pl.ds(D, 16), pl.ds(k * B, B)] = block.astype(BF)

    def turn(rows, rows_t, norm, at):
        turned = rows.astype(F32).T
        rows_t[pl.ds(0, D), pl.ds(pl.multiple_of(at * B, B), B)] = turned.astype(BF)
        norm[pl.ds(at, 1), :] = jnp.sum(turned * turned, axis=0, keepdims=True) * (0.5 / D)

    def turn_targets(k, carry):
        rows = tgt_ref[pl.ds(pl.multiple_of(k * B, B), B), :]
        tgt_one[pl.ds(pl.multiple_of(k * B, B), B), pl.ds(0, D)] = rows
        turn(rows, tgt_t, tgt_norm, k)
        return carry

    lax.fori_loop(0, NB, turn_targets, 0)
    put_bias(tgt_t, tgt_norm[...] * (-LOG2E / (EPS * SCALE)))

    def with_ones(rows):
        return jnp.concatenate([rows, ones], axis=1)

    def first_rows(at):
        rows = codes[at]
        turn(rows, src_t, src_norm, at)
        vec[0, pl.ds(at, 1), :] = lse_block(with_ones(rows), tgt_t[...])

    first_rows(tgt_me)
    for d in range(1, Q):
        gather_hi(d).wait_recv()
        for k in range(1, Q):
            gather_lo(d, k).start()

    def first_group(d, carry):
        hi = (t_hi - d + Q) % Q

        @pl.when(d > 0)
        def _():
            first_rows(hi * Q + t_lo)

        for k in range(1, Q):
            gather_lo(d, k).wait_recv()
            first_rows(hi * Q + (t_lo - k + Q) % Q)
        return carry

    lax.fori_loop(0, Q, first_group, 0)

    def combine(buf):
        high = jnp.maximum(jnp.maximum(buf[0], buf[1]), jnp.maximum(buf[2], buf[3]))
        total = jnp.exp2(buf[0] - high) + jnp.exp2(buf[1] - high)
        total = total + jnp.exp2(buf[2] - high) + jnp.exp2(buf[3] - high)
        return high + jnp.log2(total)

    def exchange(e, axis):
        hi, lo = (s_hi, s_lo) if axis == "src" else (t_hi, t_lo)
        for phase, (buf, mine, peer) in enumerate(((lo_buf, lo, lo_peer), (hi_buf, hi, hi_peer))):
            copies = [
                copy(
                    vec.at[2 * e + phase], buf.at[e, mine],
                    e_send.at[e, phase, k - 1], e_recv.at[e, phase, k - 1], peer(axis, k),
                )
                for k in range(1, Q)
            ]
            for c in copies:
                c.start()
            buf[e, mine] = vec[2 * e + phase]
            for c in copies:
                c.wait_recv()
            total = combine(buf[e])
            if phase == 0:
                vec[2 * e + 1] = total
            for c in copies:
                c.wait_send()
        return total

    def row_pass(e):
        def body(k, carry):
            vec[2 * e, pl.ds(k, 1), :] = lse_block(with_ones(codes[k]), tgt_t[...])
            return carry

        lax.fori_loop(0, NB, body, 0)

    def col_pass(e):
        def body(k, carry):
            rows = tgt_ref[pl.ds(pl.multiple_of(k * B, B), B), :]
            vec[2 * e, pl.ds(k, 1), :] = lse_block(with_ones(rows), src_t[...])
            return carry

        lax.fori_loop(0, NB, body, 0)

    slm = slm_ref[...] * LOG2E
    tlm = tlm_ref[...] * LOG2E
    back = EPS / LOG2E
    for it in range(2):
        if it > 0:
            row_pass(2 * it)
        src_log = slm - exchange(2 * it, "tgt")
        put_bias(src_t, src_log * (1.0 / SCALE))
        col_pass(2 * it + 1)
        tgt_log = tlm - exchange(2 * it + 1, "src")
        put_bias(tgt_t, tgt_log * (1.0 / SCALE))
    sd_ref[...] = src_log * back + src_norm[...]
    td_ref[...] = tgt_log * back + tgt_norm[...]

    def moments(at):
        u = jnp.dot(with_ones(codes[at]), tgt_t[...], preferred_element_type=F32)
        high = jnp.max(tile_high(u), axis=1, keepdims=True)
        w = jnp.exp2((u - high) * SCALE)
        w_hi = w.astype(BF)
        w_lo = (w - w_hi.astype(F32)).astype(BF)
        rhs = tgt_one[...]
        mom = jnp.dot(w_hi, rhs, preferred_element_type=F32) + jnp.dot(w_lo, rhs, preferred_element_type=F32)
        mass = mom[:, D:]
        return mom[:, :D] / mass, (high * SCALE + jnp.log2(mass)).T[:8, :]

    def send_lo(k, z):
        return copy(part.at[k % Q, z], got.at[k - 1, z], m_send.at[k - 1, z], m_recv.at[k - 1, z], lo_peer("tgt", k))

    def last_blocks(t, carry):
        k = (t // Q + 1) % Q
        z = t % Q
        mean, level = moments(z * Q + (t_lo + k) % Q)
        part[k, z, pl.ds(0, B), :] = mean
        part[k, z, pl.ds(B, 8), :] = level

        @pl.when(k > 0)
        def _():
            copy(
                part.at[k, z], got.at[jnp.maximum(k, 1) - 1, z], m_send.at[jnp.maximum(k, 1) - 1, z],
                m_recv.at[jnp.maximum(k, 1) - 1, z], {"tgt": t_hi * Q + (t_lo + jnp.maximum(k, 1)) % Q},
            ).start()

        return carry

    lax.fori_loop(0, NB, last_blocks, 0)

    def join(pieces):
        levels = [p[pl.ds(B, 8), :] for p in pieces]
        high = functools.reduce(jnp.maximum, levels)
        scaled = [jnp.exp2(v - high) for v in levels]
        total = functools.reduce(jnp.add, scaled)
        out = None
        for p, v in zip(pieces, scaled):
            share = jnp.broadcast_to((v / total)[:1, :], (B, B)).T
            term = p[pl.ds(0, B), :] * share
            out = term if out is None else out + term
        return out, high + jnp.log2(total)

    def send_hi(k):
        return copy(part2.at[k], got2.at[k - 1], r_send.at[k - 1], r_recv.at[k - 1], hi_peer("tgt", k))

    for k in (1, 2, 3, 0):
        z = (t_hi + k) % Q
        for j in range(1, Q):
            send_lo(j, z).wait_recv()
        mean, level = join([part.at[0, z]] + [got.at[j, z] for j in range(Q - 1)])
        part2[k, pl.ds(0, B), :] = mean
        part2[k, pl.ds(B, 8), :] = level
        if k > 0:
            send_hi(k).start()
    for k in range(1, Q):
        send_hi(k).wait_recv()
    mean, level = join([part2.at[0]] + [got2.at[j] for j in range(Q - 1)])
    map_ref[...] = mean

    for k in range(1, Q):
        gather_hi(k).wait_send()
        send_hi(k).wait_send()
        for d in range(Q):
            gather_lo(d, k).wait_send()
            send_lo(k, d).wait_send()


def shards(sources, targets, src_logmass, tgt_logmass):
    vmem = pl.BlockSpec(memory_space=pltpu.VMEM)
    dma = pltpu.SemaphoreType.DMA
    mapped, src_dual, tgt_dual = pl.pallas_call(
        kernel,
        out_shape=(
            jax.ShapeDtypeStruct((B, D), F32),
            jax.ShapeDtypeStruct((NB, B), F32),
            jax.ShapeDtypeStruct((NB, B), F32),
        ),
        in_specs=[vmem] * 4,
        out_specs=(vmem, vmem, vmem),
        scratch_shapes=[
            pltpu.VMEM((NB, B, D), BF),
            pltpu.VMEM((2 * D, N), BF),
            pltpu.VMEM((2 * D, N), BF),
            pltpu.VMEM((N, 2 * D), BF),
            pltpu.VMEM((NB, B), F32),
            pltpu.VMEM((NB, B), F32),
            pltpu.VMEM((8, NB, B), F32),
            pltpu.VMEM((4, Q, NB, B), F32),
            pltpu.VMEM((4, Q, NB, B), F32),
            pltpu.VMEM((Q, Q, B + 8, D), F32),
            pltpu.VMEM((Q - 1, Q, B + 8, D), F32),
            pltpu.VMEM((Q, B + 8, D), F32),
            pltpu.VMEM((Q - 1, B + 8, D), F32),
            dma((Q - 1,)), dma((Q - 1,)), dma((Q, Q - 1)), dma((Q, Q - 1)),
            dma((4, 2, Q - 1)), dma((4, 2, Q - 1)),
            dma((Q - 1, Q)), dma((Q - 1, Q)), dma((Q - 1,)), dma((Q - 1,)),
        ],
        compiler_params=pltpu.CompilerParams(
            collective_id=0, has_side_effects=True, vmem_limit_bytes=48 * 1024 * 1024
        ),
    )(sources, targets, src_logmass.reshape(NB, B), tgt_logmass.reshape(NB, B))
    return mapped, src_dual.reshape(N), tgt_dual.reshape(N)


def solution(mesh):
    return jax.shard_map(
        shards,
        mesh=mesh,
        in_specs=(P(("src", "tgt"), None), P("tgt", None), P("src"), P("tgt")),
        out_specs=(P(("src", "tgt"), None), P("src"), P("tgt")),
        check_vma=False,
    )
```

```python
import functools
import math

import jax
import jax.numpy as jnp
from jax import lax
from jax.experimental import pallas as pl
from jax.experimental.pallas import tpu as pltpu
from jax.sharding import PartitionSpec as P

MESH = pl.DeviceIdType.MESH
EPS = 0.03125
LOG2E = math.log2(math.e)
B = 128
NB = 16
N = B * NB
D = 128
Q = 4
SCALE = LOG2E / (D * EPS)
BF = jnp.bfloat16
F32 = jnp.float32


GROUP = 16


def fold(x, op):
    x = op(x.reshape(x.shape[0] // GROUP, GROUP, x.shape[1]), axis=0)
    half = GROUP // 2
    return jnp.maximum(x[:half], x[half:]) if op is jnp.max else x[:half] + x[half:]


def lse_tile(rows, bias, rhs):
    high = None
    for q in range(NB):
        at = pl.ds(q * B, B)
        u = jnp.dot(jnp.concatenate([rows[at, :], bias[at, :]], axis=1), rhs, preferred_element_type=F32)
        new = fold(u, jnp.max)
        if high is not None:
            new = jnp.maximum(high, new)
        part = jnp.exp2((u.reshape(B // 8, 8, u.shape[1]) - new[None]) * SCALE).reshape(u.shape)
        part = fold(part, jnp.sum)
        total = part if high is None else total * jnp.exp2((high - new) * SCALE) + part
        high = new
    y = high * SCALE + jnp.log2(total)
    top = jnp.max(y, axis=0, keepdims=True)
    return top + jnp.log2(jnp.sum(jnp.exp2(y - top), axis=0, keepdims=True))


CHUNK = 256
UNROLL = 8


def moment_tile(rows, rows_t, bias, rhs):
    high = None
    for q in range(N // CHUNK):
        at = pl.ds(q * CHUNK, CHUNK)
        u = jnp.dot(jnp.concatenate([rows[at, :], bias[at, :]], axis=1), rhs, preferred_element_type=F32)
        new = jnp.max(fold(u, jnp.max), axis=0, keepdims=True)
        if high is not None:
            new = jnp.maximum(high, new)
        w = jnp.exp2((u - new) * SCALE)
        mass_part = fold(w, jnp.sum)
        w_hi = w.astype(BF)
        w_lo = (w - w_hi.astype(F32)).astype(BF)
        lhs = rows_t[:, at]
        part = jnp.dot(lhs, w_hi, preferred_element_type=F32) + jnp.dot(lhs, w_lo, preferred_element_type=F32)
        if high is None:
            total, mass = part, mass_part
        else:
            ratio = jnp.exp2((high - new) * SCALE)
            total, mass = total * ratio + part, mass * ratio + mass_part
        high = new
    mass = jnp.sum(mass, axis=0, keepdims=True)
    return total / mass, jnp.broadcast_to(high * SCALE + jnp.log2(mass), (8, rhs.shape[1]))


def kernel(
    src_ref, tgt_ref, slm_ref, tlm_ref, map_ref, sd_ref, td_ref,
    codes, src_t, tgt_t, src_bias, tgt_bias, src_norm, tgt_norm, vec, lo_buf, hi_buf,
    part, got, part2, got2,
    g_hi_send, g_hi_recv, g_lo_send, g_lo_recv,
    e_send, e_recv, m_send, m_recv, r_send, r_recv,
):
    src_me = lax.axis_index("src")
    tgt_me = lax.axis_index("tgt")
    s_hi, s_lo = src_me // Q, src_me % Q
    t_hi, t_lo = tgt_me // Q, tgt_me % Q

    def lo_peer(axis, k):
        hi, lo = (s_hi, s_lo) if axis == "src" else (t_hi, t_lo)
        return {axis: hi * Q + (lo + k) % Q}

    def hi_peer(axis, k):
        hi, lo = (s_hi, s_lo) if axis == "src" else (t_hi, t_lo)
        return {axis: ((hi + k) % Q) * Q + lo}

    barrier = pltpu.get_barrier_semaphore()
    for axis in ("tgt", "src"):
        for k in range(1, Q):
            pl.semaphore_signal(barrier, 1, device_id=lo_peer(axis, k), device_id_type=MESH)
            pl.semaphore_signal(barrier, 1, device_id=hi_peer(axis, k), device_id_type=MESH)

    def copy(src, dst, send, recv, peer):
        return pltpu.make_async_remote_copy(
            src_ref=src, dst_ref=dst, send_sem=send, recv_sem=recv, device_id=peer, device_id_type=MESH
        )

    def block_at(k):
        return pl.ds(pl.multiple_of(k * B, B), B)

    codes[block_at(tgt_me), :] = src_ref[...]
    pl.semaphore_wait(barrier, 4 * (Q - 1))

    def gather_hi(k):
        return copy(src_ref, codes.at[block_at(tgt_me), :], g_hi_send.at[k - 1], g_hi_recv.at[k - 1], hi_peer("tgt", k))

    def gather_lo(d, k):
        block = ((t_hi - d + Q) % Q) * Q + t_lo
        src = src_ref if isinstance(d, int) and d == 0 else codes.at[block_at(block), :]
        return copy(src, codes.at[block_at(block), :], g_lo_send.at[d, k - 1], g_lo_recv.at[d, k - 1], lo_peer("tgt", k))

    for k in range(1, Q):
        gather_hi(k).start()
    for k in range(1, Q):
        gather_lo(0, k).start()

    lane = lax.broadcasted_iota(jnp.int32, (B, B), 1)
    ones = jnp.ones((D, 2 * B), BF)

    def put_bias(out, bias):
        hi = bias.astype(BF).astype(F32)
        rest = bias - hi
        mid = rest.astype(BF).astype(F32)
        low = rest - mid
        turned = jnp.concatenate([hi, mid, low, jnp.zeros((B - 3 * NB, B), F32)], axis=0).T
        for k in range(NB):
            out[pl.ds(k * B, B), :] = jnp.where(lane % NB == k, turned, 0.0).astype(BF)

    def turn(rows, rows_t, norm, at):
        turned = rows.astype(F32).T
        rows_t[:, block_at(at)] = turned.astype(BF)
        norm[pl.ds(at, 1), :] = jnp.sum(turned * turned, axis=0, keepdims=True) * (0.5 / D)

    def under(rows_t, first, second):
        pair = jnp.concatenate([rows_t[:, block_at(first)], rows_t[:, block_at(second)]], axis=1)
        return jnp.concatenate([pair, ones], axis=0)

    for k in range(NB):
        turn(tgt_ref[pl.ds(k * B, B), :], tgt_t, tgt_norm, k)
    put_bias(tgt_bias, tgt_norm[...] * (-LOG2E / (EPS * SCALE)))

    def take(at):
        turn(codes[block_at(at), :], src_t, src_norm, at)

    def first_pair(first, second):
        total = lse_tile(tgt_ref, tgt_bias, under(src_t, first, second))
        vec[0, pl.ds(first, 1), :] = total[:, :B]
        vec[0, pl.ds(second, 1), :] = total[:, B:]

    for d in range(1, Q):
        gather_hi(d).wait_recv()
        for k in range(1, Q):
            gather_lo(d, k).start()

    def first_group(d, carry):
        hi = (t_hi - d + Q) % Q
        at = [hi * Q + (t_lo - k + Q) % Q for k in range(Q)]
        take(at[0])
        gather_lo(d, 1).wait_recv()
        take(at[1])
        first_pair(at[0], at[1])
        gather_lo(d, 2).wait_recv()
        take(at[2])
        gather_lo(d, 3).wait_recv()
        take(at[3])
        first_pair(at[2], at[3])
        return carry

    lax.fori_loop(0, Q, first_group, 0)

    def combine(buf):
        high = jnp.maximum(jnp.maximum(buf[0], buf[1]), jnp.maximum(buf[2], buf[3]))
        total = jnp.exp2(buf[0] - high) + jnp.exp2(buf[1] - high)
        total = total + jnp.exp2(buf[2] - high) + jnp.exp2(buf[3] - high)
        return high + jnp.log2(total)

    def exchange(e, axis):
        hi, lo = (s_hi, s_lo) if axis == "src" else (t_hi, t_lo)
        for phase, (buf, mine, peer) in enumerate(((lo_buf, lo, lo_peer), (hi_buf, hi, hi_peer))):
            copies = [
                copy(
                    vec.at[2 * e + phase], buf.at[e, mine],
                    e_send.at[e, phase, k - 1], e_recv.at[e, phase, k - 1], peer(axis, k),
                )
                for k in range(1, Q)
            ]
            for c in copies:
                c.start()
            buf[e, mine] = vec[2 * e + phase]
            for c in copies:
                c.wait_recv()
            total = combine(buf[e])
            if phase == 0:
                vec[2 * e + 1] = total
            for c in copies:
                c.wait_send()
        return total

    def whole_pass(e, rows, bias, rows_t):
        def body(k, carry):
            total = lse_tile(rows, bias, under(rows_t, 2 * k, 2 * k + 1))
            vec[2 * e, pl.ds(2 * k, 1), :] = total[:, :B]
            vec[2 * e, pl.ds(2 * k + 1, 1), :] = total[:, B:]
            return carry

        lax.fori_loop(0, NB // 2, body, 0, unroll=UNROLL)

    slm = slm_ref[...] * LOG2E
    tlm = tlm_ref[...] * LOG2E
    back = EPS / LOG2E
    for it in range(2):
        if it > 0:
            whole_pass(2 * it, tgt_ref, tgt_bias, src_t)
        src_log = slm - exchange(2 * it, "tgt")
        put_bias(src_bias, src_log * (1.0 / SCALE))
        whole_pass(2 * it + 1, codes, src_bias, tgt_t)
        tgt_log = tlm - exchange(2 * it + 1, "src")
        put_bias(tgt_bias, tgt_log * (1.0 / SCALE))
    sd_ref[...] = src_log * back + src_norm[...]
    td_ref[...] = tgt_log * back + tgt_norm[...]

    def send_lo(k, z):
        return copy(part.at[k % Q, z], got.at[k - 1, z], m_send.at[k - 1, z], m_recv.at[k - 1, z], lo_peer("tgt", k))

    def last_group(t, carry):
        k = (t + 1) % Q
        x = (t_lo + k) % Q
        for z in range(0, Q, 2):
            mean, level = moment_tile(tgt_ref, tgt_t, tgt_bias, under(src_t, z * Q + x, (z + 1) * Q + x))
            for j in range(2):
                part[k, z + j, pl.ds(0, B), :] = mean[:, j * B : (j + 1) * B]
                part[k, z + j, pl.ds(B, 8), :] = level[:, j * B : (j + 1) * B]

        @pl.when(k > 0)
        def _():
            near = jnp.maximum(k, 1)
            for z in range(Q):
                copy(
                    part.at[k, z], got.at[near - 1, z], m_send.at[near - 1, z],
                    m_recv.at[near - 1, z], {"tgt": t_hi * Q + (t_lo + near) % Q},
                ).start()

        return carry

    lax.fori_loop(0, Q, last_group, 0)

    def join(pieces):
        levels = [p[pl.ds(B, 8), :] for p in pieces]
        high = functools.reduce(jnp.maximum, levels)
        scaled = [jnp.exp2(v - high) for v in levels]
        total = functools.reduce(jnp.add, scaled)
        out = None
        for p, v in zip(pieces, scaled):
            term = p[pl.ds(0, B), :] * (v / total)[:1, :]
            out = term if out is None else out + term
        return out, high + jnp.log2(total)

    def send_hi(k):
        return copy(part2.at[k], got2.at[k - 1], r_send.at[k - 1], r_recv.at[k - 1], hi_peer("tgt", k))

    for k in (1, 2, 3, 0):
        z = (t_hi + k) % Q
        for j in range(1, Q):
            send_lo(j, z).wait_recv()
        mean, level = join([part.at[0, z]] + [got.at[j, z] for j in range(Q - 1)])
        part2[k, pl.ds(0, B), :] = mean
        part2[k, pl.ds(B, 8), :] = level
        if k > 0:
            send_hi(k).start()
    for k in range(1, Q):
        send_hi(k).wait_recv()
    mean, level = join([part2.at[0]] + [got2.at[j] for j in range(Q - 1)])
    map_ref[...] = mean.T

    for k in range(1, Q):
        gather_hi(k).wait_send()
        send_hi(k).wait_send()
        for d in range(Q):
            gather_lo(d, k).wait_send()
            send_lo(k, d).wait_send()


def shards(sources, targets, src_logmass, tgt_logmass):
    vmem = pl.BlockSpec(memory_space=pltpu.VMEM)
    dma = pltpu.SemaphoreType.DMA
    mapped, src_dual, tgt_dual = pl.pallas_call(
        kernel,
        out_shape=(
            jax.ShapeDtypeStruct((B, D), F32),
            jax.ShapeDtypeStruct((NB, B), F32),
            jax.ShapeDtypeStruct((NB, B), F32),
        ),
        in_specs=[vmem] * 4,
        out_specs=(vmem, vmem, vmem),
        scratch_shapes=[
            pltpu.VMEM((N, D), BF),
            pltpu.VMEM((D, N), BF),
            pltpu.VMEM((D, N), BF),
            pltpu.VMEM((N, B), BF),
            pltpu.VMEM((N, B), BF),
            pltpu.VMEM((NB, B), F32),
            pltpu.VMEM((NB, B), F32),
            pltpu.VMEM((8, NB, B), F32),
            pltpu.VMEM((4, Q, NB, B), F32),
            pltpu.VMEM((4, Q, NB, B), F32),
            pltpu.VMEM((Q, Q, B + 8, D), F32),
            pltpu.VMEM((Q - 1, Q, B + 8, D), F32),
            pltpu.VMEM((Q, B + 8, D), F32),
            pltpu.VMEM((Q - 1, B + 8, D), F32),
            dma((Q - 1,)), dma((Q - 1,)), dma((Q, Q - 1)), dma((Q, Q - 1)),
            dma((4, 2, Q - 1)), dma((4, 2, Q - 1)),
            dma((Q - 1, Q)), dma((Q - 1, Q)), dma((Q - 1,)), dma((Q - 1,)),
        ],
        compiler_params=pltpu.CompilerParams(
            collective_id=0, has_side_effects=True, vmem_limit_bytes=48 * 1024 * 1024
        ),
    )(sources, targets, src_logmass.reshape(NB, B), tgt_logmass.reshape(NB, B))
    return mapped, src_dual.reshape(N), tgt_dual.reshape(N)


def solution(mesh):
    return jax.shard_map(
        shards,
        mesh=mesh,
        in_specs=(P(("src", "tgt"), None), P("tgt", None), P("src"), P("tgt")),
        out_specs=(P(("src", "tgt"), None), P("src"), P("tgt")),
        check_vma=False,
    )
```

```python
import functools
import math

import jax
import jax.numpy as jnp
from jax import lax
from jax.experimental import pallas as pl
from jax.experimental.pallas import tpu as pltpu
from jax.sharding import PartitionSpec as P

MESH = pl.DeviceIdType.MESH
EPS = 0.03125
LOG2E = math.log2(math.e)
B = 128
NB = 16
N = B * NB
D = 128
Q = 4
SCALE = LOG2E / (D * EPS)
BF = jnp.bfloat16
F32 = jnp.float32


FILL = 7250
GROUP = 16


def fold(x, op):
    x = op(x.reshape(x.shape[0] // GROUP, GROUP, x.shape[1]), axis=0)
    half = GROUP // 2
    return jnp.maximum(x[:half], x[half:]) if op is jnp.max else x[:half] + x[half:]


def lse_tile(rows, bias, rhs):
    high = None
    for q in range(NB):
        at = pl.ds(q * B, B)
        u = jnp.dot(jnp.concatenate([rows[at, :], bias[at, :]], axis=1), rhs, preferred_element_type=F32)
        new = fold(u, jnp.max)
        if high is not None:
            new = jnp.maximum(high, new)
        part = jnp.exp2((u.reshape(B // 8, 8, u.shape[1]) - new[None]) * SCALE).reshape(u.shape)
        part = fold(part, jnp.sum)
        total = part if high is None else total * jnp.exp2((high - new) * SCALE) + part
        high = new
    y = high * SCALE + jnp.log2(total)
    top = jnp.max(y, axis=0, keepdims=True)
    return top + jnp.log2(jnp.sum(jnp.exp2(y - top), axis=0, keepdims=True))


CHUNK = 256
UNROLL = 4


def moment_tile(rows, rows_t, bias, rhs):
    high = None
    for q in range(N // CHUNK):
        at = pl.ds(q * CHUNK, CHUNK)
        u = jnp.dot(jnp.concatenate([rows[at, :], bias[at, :]], axis=1), rhs, preferred_element_type=F32)
        new = jnp.max(fold(u, jnp.max), axis=0, keepdims=True)
        if high is not None:
            new = jnp.maximum(high, new)
        w = jnp.exp2((u - new) * SCALE)
        mass_part = fold(w, jnp.sum)
        w_hi = w.astype(BF)
        w_lo = (w - w_hi.astype(F32)).astype(BF)
        lhs = rows_t[:, at]
        part = jnp.dot(lhs, w_hi, preferred_element_type=F32) + jnp.dot(lhs, w_lo, preferred_element_type=F32)
        if high is None:
            total, mass = part, mass_part
        else:
            ratio = jnp.exp2((high - new) * SCALE)
            total, mass = total * ratio + part, mass * ratio + mass_part
        high = new
    mass = jnp.sum(mass, axis=0, keepdims=True)
    return total / mass, jnp.broadcast_to(high * SCALE + jnp.log2(mass), (8, rhs.shape[1]))


def kernel(
    src_hbm, tgt_hbm, slm_hbm, tlm_hbm, map_ref, sd_ref, td_ref,
    rows, rows_t, bias, logmass, norm, dual, vec, inbox,
    part, got, part2, got2, in_sem,
    g_hi_send, g_hi_recv, g_lo_send, g_lo_recv,
    e_send, e_recv, m_send, m_recv, r_send, r_recv,
):
    src_me = lax.axis_index("src")
    tgt_me = lax.axis_index("tgt")
    s_hi, s_lo = src_me // Q, src_me % Q
    t_hi, t_lo = tgt_me // Q, tgt_me % Q

    def lo_peer(axis, k):
        hi, lo = (s_hi, s_lo) if axis == "src" else (t_hi, t_lo)
        return {axis: hi * Q + (lo + k) % Q}

    def hi_peer(axis, k):
        hi, lo = (s_hi, s_lo) if axis == "src" else (t_hi, t_lo)
        return {axis: ((hi + k) % Q) * Q + lo}

    codes, src_t, src_norm = rows.at[0], rows_t.at[0], norm.at[0]
    tgt_ref, tgt_t, tgt_norm, tgt_bias = rows.at[1], rows_t.at[1], norm.at[1], bias.at[1]

    def block_at(k):
        return pl.ds(pl.multiple_of(k * B, B), B)

    fetches = [
        pltpu.make_async_copy(src, dst, in_sem.at[i])
        for i, (src, dst) in enumerate((
            (src_hbm, codes.at[block_at(tgt_me), :]), (tgt_hbm, tgt_ref), (slm_hbm, logmass.at[0]), (tlm_hbm, logmass.at[1]),
        ))
    ]
    for f in fetches:
        f.start()

    barrier = pltpu.get_barrier_semaphore()
    for k in range(1, NB):
        for axis, me in (("tgt", tgt_me), ("src", src_me)):
            pl.semaphore_signal(barrier, 1, device_id={axis: (me + k) % NB}, device_id_type=MESH)

    def copy(src, dst, send, recv, peer):
        return pltpu.make_async_remote_copy(
            src_ref=src, dst_ref=dst, send_sem=send, recv_sem=recv, device_id=peer, device_id_type=MESH
        )

    def gather_hi(k):
        own = codes.at[block_at(tgt_me), :]
        return copy(own, own, g_hi_send.at[k - 1], g_hi_recv.at[k - 1], hi_peer("tgt", k))

    def gather_lo(d, k):
        block = ((t_hi - d + Q) % Q) * Q + t_lo
        rows = codes.at[block_at(block), :]
        return copy(rows, rows, g_lo_send.at[d, k - 1], g_lo_recv.at[d, k - 1], lo_peer("tgt", k))

    lane = lax.broadcasted_iota(jnp.int32, (B, B), 1)
    ones = jnp.ones((D, 2 * B), BF)

    def put_bias(out, bias):
        hi = bias.astype(BF).astype(F32)
        rest = bias - hi
        mid = rest.astype(BF).astype(F32)
        low = rest - mid
        turned = jnp.concatenate([hi, mid, low, jnp.zeros((B - 3 * NB, B), F32)], axis=0).T
        for k in range(NB):
            out[pl.ds(k * B, B), :] = jnp.where(lane % NB == k, turned, 0.0).astype(BF)

    def turn(rows, rows_t, norm, at):
        turned = rows.astype(F32).T
        rows_t[:, block_at(at)] = turned.astype(BF)
        norm[pl.ds(at, 1), :] = jnp.sum(turned * turned, axis=0, keepdims=True) * (0.5 / D)

    def under(rows_t, first, second):
        pair = jnp.concatenate([rows_t[:, block_at(first)], rows_t[:, block_at(second)]], axis=1)
        return jnp.concatenate([pair, ones], axis=0)

    fetches[0].wait()
    pl.semaphore_wait(barrier, 2 * (NB - 1))
    for k in range(1, Q):
        gather_hi(k).start()
    for k in range(1, Q):
        gather_lo(0, k).start()

    for f in fetches[1:]:
        f.wait()
    for k in range(NB):
        turn(tgt_ref[pl.ds(k * B, B), :], tgt_t, tgt_norm, k)
    put_bias(tgt_bias, tgt_norm[...] * (-LOG2E / (EPS * SCALE)))

    def take(at):
        turn(codes[block_at(at), :], src_t, src_norm, at)

    def first_pair(first, second):
        total = lse_tile(tgt_ref, tgt_bias, under(src_t, first, second))
        vec[0, first // 8, pl.ds(first % 8, 1), :] = total[:, :B]
        vec[0, second // 8, pl.ds(second % 8, 1), :] = total[:, B:]

    for d in range(1, Q):
        gather_hi(d).wait_recv()
        for k in range(1, Q):
            gather_lo(d, k).start()

    def first_group(d, carry):
        hi = (t_hi - d + Q) % Q
        at = [hi * Q + (t_lo - k + Q) % Q for k in range(Q)]
        take(at[0])
        gather_lo(d, 1).wait_recv()
        take(at[1])
        first_pair(at[0], at[1])
        gather_lo(d, 2).wait_recv()
        take(at[2])
        gather_lo(d, 3).wait_recv()
        take(at[3])
        first_pair(at[2], at[3])
        return carry

    lax.fori_loop(0, Q, first_group, 0)

    def message(e, h, k):
        odd = e % 2
        peer = ((src_me + odd * k) % NB, (tgt_me + (1 - odd) * k) % NB)
        mine = odd * src_me + (1 - odd) * tgt_me
        return copy(vec.at[e, h], inbox.at[e, h, mine], e_send.at[e, h], e_recv.at[e, h], peer)

    def send_half(e, h):
        for k in range(1, NB):
            message(e, h, k).start()
        inbox[e, h, (e % 2) * src_me + (1 - e % 2) * tgt_me] = vec[e, h]

    def all_bytes(e, h, sem):
        others = inbox.at[e, h, pl.ds(0, NB - 1)]
        return pltpu.make_async_copy(others, others, sem.at[e, h])

    def receive(e):
        for h in range(2):
            all_bytes(e, h, e_recv).wait()
        pieces = [inbox[e, :, k].reshape(NB, B) for k in range(NB)]
        high = functools.reduce(jnp.maximum, pieces)
        level = high + jnp.log2(functools.reduce(jnp.add, [jnp.exp2(p - high) for p in pieces]))
        side = e % 2
        log = logmass[side] * LOG2E - level
        put_bias(bias.at[side], log * (1.0 / SCALE))
        dual[side] = log * (EPS / LOG2E) + norm[side]

    def whole_pass(e, carry):
        receive(e - 1)
        side = (e - 1) % 2

        def half(h, carry):
            def body(k, carry):
                at = h * (NB // 4) + k
                total = lse_tile(rows.at[side], bias.at[side], under(rows_t.at[1 - side], 2 * at, 2 * at + 1))
                vec[e, h, pl.ds(2 * k, 1), :] = total[:, :B]
                vec[e, h, pl.ds(2 * k + 1, 1), :] = total[:, B:]
                return carry

            lax.fori_loop(0, NB // 4, body, 0, unroll=UNROLL)
            send_half(e, h)
            return carry

        return lax.fori_loop(0, 2, half, carry)

    send_half(0, 0)
    send_half(0, 1)
    lax.fori_loop(1, 4, whole_pass, 0)
    receive(3)
    sd_ref[...] = dual[0]
    td_ref[...] = dual[1]

    def send_lo(k, z):
        return copy(part.at[k % Q, z], got.at[k - 1, z], m_send.at[k - 1, z], m_recv.at[k - 1, z], lo_peer("tgt", k))

    def last_group(t, carry):
        k = (t + 1) % Q
        x = (t_lo + k) % Q
        near = jnp.maximum(k, 1)
        for z in range(0, Q, 2):
            mean, level = moment_tile(tgt_ref, tgt_t, tgt_bias, under(src_t, z * Q + x, (z + 1) * Q + x))
            for j in range(2):
                part[k, z + j, pl.ds(0, B), :] = mean[:, j * B : (j + 1) * B]
                part[k, z + j, pl.ds(B, 8), :] = level[:, j * B : (j + 1) * B]

            @pl.when(k > 0)
            def _():
                for j in range(z, z + 2):
                    copy(
                        part.at[k, j], got.at[near - 1, j], m_send.at[near - 1, j],
                        m_recv.at[near - 1, j], {"tgt": t_hi * Q + (t_lo + near) % Q},
                    ).start()

        return carry

    lax.fori_loop(0, Q, last_group, 0)

    def join(pieces):
        levels = [p[pl.ds(B, 8), :] for p in pieces]
        high = functools.reduce(jnp.maximum, levels)
        scaled = [jnp.exp2(v - high) for v in levels]
        total = functools.reduce(jnp.add, scaled)
        out = None
        for p, v in zip(pieces, scaled):
            term = p[pl.ds(0, B), :] * (v / total)[:1, :]
            out = term if out is None else out + term
        return out, high + jnp.log2(total)

    def send_hi(k):
        return copy(part2.at[k], got2.at[k - 1], r_send.at[k - 1], r_recv.at[k - 1], hi_peer("tgt", k))

    for k in (1, 2, 3, 0):
        z = (t_hi + k) % Q
        for j in range(1, Q):
            send_lo(j, z).wait_recv()
        mean, level = join([part.at[0, z]] + [got.at[j, z] for j in range(Q - 1)])
        part2[k, pl.ds(0, B), :] = mean
        part2[k, pl.ds(B, 8), :] = level
        if k > 0:
            send_hi(k).start()
    for k in range(1, Q):
        send_hi(k).wait_recv()
    mean, level = join([part2.at[0]] + [got2.at[j] for j in range(Q - 1)])
    map_ref[...] = mean.T

    for k in range(1, Q):
        gather_hi(k).wait_send()
        send_hi(k).wait_send()
        for d in range(Q):
            gather_lo(d, k).wait_send()
            send_lo(k, d).wait_send()
    for e in range(4):
        for h in range(2):
            all_bytes(e, h, e_send).wait()


def shards(sources, targets, src_logmass, tgt_logmass):
    vmem = pl.BlockSpec(memory_space=pltpu.VMEM)
    dma = pltpu.SemaphoreType.DMA
    mapped, src_dual, tgt_dual = pl.pallas_call(
        kernel,
        out_shape=(
            jax.ShapeDtypeStruct((B, D), F32),
            jax.ShapeDtypeStruct((NB, B), F32),
            jax.ShapeDtypeStruct((NB, B), F32),
        ),
        in_specs=[pl.BlockSpec(memory_space=pltpu.HBM)] * 4,
        out_specs=(vmem, vmem, vmem),
        scratch_shapes=[
            pltpu.VMEM((2, N, D), BF),
            pltpu.VMEM((2, D, N), BF),
            pltpu.VMEM((2, N, B), BF),
            pltpu.VMEM((FILL, NB, B), F32),
            pltpu.VMEM((2, NB, B), F32),
            pltpu.VMEM((2, NB, B), F32),
            pltpu.VMEM((4, 2, NB // 2, B), F32),
            pltpu.VMEM((4, 2, NB, NB // 2, B), F32),
            pltpu.VMEM((Q, Q, B + 8, D), F32),
            pltpu.VMEM((Q - 1, Q, B + 8, D), F32),
            pltpu.VMEM((Q, B + 8, D), F32),
            pltpu.VMEM((Q - 1, B + 8, D), F32),
            dma((4,)),
            dma((Q - 1,)), dma((Q - 1,)), dma((Q, Q - 1)), dma((Q, Q - 1)),
            dma((4, 2)), dma((4, 2)),
            dma((Q - 1, Q)), dma((Q - 1, Q)), dma((Q - 1,)), dma((Q - 1,)),
        ],
        compiler_params=pltpu.CompilerParams(
            collective_id=0, has_side_effects=True, vmem_limit_bytes=64 * 1024 * 1024
        ),
    )(sources, targets, src_logmass.reshape(NB, B), tgt_logmass.reshape(NB, B))
    return mapped, src_dual.reshape(N), tgt_dual.reshape(N)


def solution(mesh):
    return jax.shard_map(
        shards,
        mesh=mesh,
        in_specs=(P(("src", "tgt"), None), P("tgt", None), P("src"), P("tgt")),
        out_specs=(P(("src", "tgt"), None), P("src"), P("tgt")),
        check_vma=False,
    )
```

```python
import functools
import math

import jax
import jax.numpy as jnp
from jax import lax
from jax.experimental import pallas as pl
from jax.experimental.pallas import tpu as pltpu
from jax.sharding import PartitionSpec as P

MESH = pl.DeviceIdType.MESH
EPS = 0.03125
LOG2E = math.log2(math.e)
B = 128
NB = 16
N = B * NB
D = 128
Q = 4
SCALE = LOG2E / (D * EPS)
BF = jnp.bfloat16
F32 = jnp.float32


FILL = 6880
GROUP = 16


def fold(x, op):
    x = op(x.reshape(x.shape[0] // GROUP, GROUP, x.shape[1]), axis=0)
    half = GROUP // 2
    return jnp.maximum(x[:half], x[half:]) if op is jnp.max else x[:half] + x[half:]


def lse_tile(rows, bias, rhs):
    high = None
    for q in range(NB):
        at = pl.ds(q * B, B)
        u = jnp.dot(jnp.concatenate([rows[at, :], bias[at, :]], axis=1), rhs, preferred_element_type=F32)
        new = fold(u, jnp.max)
        if high is not None:
            new = jnp.maximum(high, new)
        part = jnp.exp2((u.reshape(B // 8, 8, u.shape[1]) - new[None]) * SCALE).reshape(u.shape)
        part = fold(part, jnp.sum)
        total = part if high is None else total * jnp.exp2((high - new) * SCALE) + part
        high = new
    y = high * SCALE + jnp.log2(total)
    top = jnp.max(y, axis=0, keepdims=True)
    return top + jnp.log2(jnp.sum(jnp.exp2(y - top), axis=0, keepdims=True))


CHUNK = 256
UNROLL = 4


def moment_step(rows, rows_t, bias, rhs, high, mass, total):
    for q in range(N // CHUNK):
        at = pl.ds(q * CHUNK, CHUNK)
        u = jnp.dot(jnp.concatenate([rows[at, :], bias[at, :]], axis=1), rhs, preferred_element_type=F32)
        new = jnp.maximum(high, jnp.max(fold(u, jnp.max), axis=0, keepdims=True))
        w = jnp.exp2((u - new) * SCALE)
        w_hi = w.astype(BF)
        w_lo = (w - w_hi.astype(F32)).astype(BF)
        lhs = rows_t[:, at]
        ratio = jnp.exp2((high - new) * SCALE)
        mass = mass * ratio + fold(w, jnp.sum)
        part = jnp.dot(lhs, w_hi, preferred_element_type=F32) + jnp.dot(lhs, w_lo, preferred_element_type=F32)
        total = total * ratio + part
        high = new
    return high, mass, total


def kernel(
    src_hbm, tgt_hbm, slm_hbm, tlm_hbm, map_ref, sd_ref, td_ref,
    rows, rows_t, bias, logmass, norm, dual, vec, inbox,
    moment, mass, high, far_bias, part, got, in_sem,
    g_hi_send, g_hi_recv, g_lo_send, g_lo_recv,
    e_send, e_recv, x_send, x_recv, f_send, f_recv, b_send, b_recv, r_send, r_recv,
):
    src_me = lax.axis_index("src")
    tgt_me = lax.axis_index("tgt")
    s_hi, s_lo = src_me // Q, src_me % Q
    t_hi, t_lo = tgt_me // Q, tgt_me % Q

    def lo_peer(axis, k):
        hi, lo = (s_hi, s_lo) if axis == "src" else (t_hi, t_lo)
        return {axis: hi * Q + (lo + k) % Q}

    def hi_peer(axis, k):
        hi, lo = (s_hi, s_lo) if axis == "src" else (t_hi, t_lo)
        return {axis: ((hi + k) % Q) * Q + lo}

    codes, src_t, src_norm = rows.at[0], rows_t.at[0], norm.at[0]
    tgt_ref, tgt_t, tgt_norm, tgt_bias = rows.at[1], rows_t.at[1], norm.at[1], bias.at[1]

    def block_at(k):
        return pl.ds(pl.multiple_of(k * B, B), B)

    fetches = [
        pltpu.make_async_copy(src, dst, in_sem.at[i])
        for i, (src, dst) in enumerate((
            (src_hbm, codes.at[block_at(tgt_me), :]), (tgt_hbm, tgt_ref), (slm_hbm, logmass.at[0]), (tlm_hbm, logmass.at[1]),
        ))
    ]
    for f in fetches:
        f.start()

    barrier = pltpu.get_barrier_semaphore()
    for k in range(1, NB):
        for axis, me in (("tgt", tgt_me), ("src", src_me)):
            pl.semaphore_signal(barrier, 1, device_id={axis: (me + k) % NB}, device_id_type=MESH)

    def copy(src, dst, send, recv, peer):
        return pltpu.make_async_remote_copy(
            src_ref=src, dst_ref=dst, send_sem=send, recv_sem=recv, device_id=peer, device_id_type=MESH
        )

    def gather_hi(k):
        own = codes.at[block_at(tgt_me), :]
        return copy(own, own, g_hi_send.at[k - 1], g_hi_recv.at[k - 1], hi_peer("tgt", k))

    def gather_lo(d, k):
        block = ((t_hi - d + Q) % Q) * Q + t_lo
        rows = codes.at[block_at(block), :]
        return copy(rows, rows, g_lo_send.at[d, k - 1], g_lo_recv.at[d, k - 1], lo_peer("tgt", k))

    lane = lax.broadcasted_iota(jnp.int32, (B, B), 1)
    ones = jnp.ones((D, 2 * B), BF)

    def put_bias(out, bias):
        hi = bias.astype(BF).astype(F32)
        rest = bias - hi
        mid = rest.astype(BF).astype(F32)
        low = rest - mid
        turned = jnp.concatenate([hi, mid, low, jnp.zeros((B - 3 * NB, B), F32)], axis=0).T
        for k in range(NB):
            out[pl.ds(k * B, B), :] = jnp.where(lane % NB == k, turned, 0.0).astype(BF)

    def turn(rows, rows_t, norm, at):
        turned = rows.astype(F32).T
        rows_t[:, block_at(at)] = turned.astype(BF)
        norm[pl.ds(at, 1), :] = jnp.sum(turned * turned, axis=0, keepdims=True) * (0.5 / D)

    def under(rows_t, first, second):
        pair = jnp.concatenate([rows_t[:, block_at(first)], rows_t[:, block_at(second)]], axis=1)
        return jnp.concatenate([pair, ones], axis=0)

    fetches[0].wait()
    pl.semaphore_wait(barrier, 2 * (NB - 1))
    for k in range(1, Q):
        gather_hi(k).start()
    for k in range(1, Q):
        gather_lo(0, k).start()

    for f in fetches[1:]:
        f.wait()
    for k in range(NB):
        turn(tgt_ref[pl.ds(k * B, B), :], tgt_t, tgt_norm, k)
    put_bias(tgt_bias, tgt_norm[...] * (-LOG2E / (EPS * SCALE)))

    def take(at):
        turn(codes[block_at(at), :], src_t, src_norm, at)

    def first_pair(first, second):
        total = lse_tile(tgt_ref, tgt_bias, under(src_t, first, second))
        vec[0, first // 8, pl.ds(first % 8, 1), :] = total[:, :B]
        vec[0, second // 8, pl.ds(second % 8, 1), :] = total[:, B:]

    for d in range(1, Q):
        gather_hi(d).wait_recv()
        for k in range(1, Q):
            gather_lo(d, k).start()

    def first_group(d, carry):
        hi = (t_hi - d + Q) % Q
        at = [hi * Q + (t_lo - k + Q) % Q for k in range(Q)]
        take(at[0])
        gather_lo(d, 1).wait_recv()
        take(at[1])
        first_pair(at[0], at[1])
        gather_lo(d, 2).wait_recv()
        take(at[2])
        gather_lo(d, 3).wait_recv()
        take(at[3])
        first_pair(at[2], at[3])
        return carry

    lax.fori_loop(0, Q, first_group, 0)

    def message(e, h, k):
        odd = e % 2
        peer = ((src_me + odd * k) % NB, (tgt_me + (1 - odd) * k) % NB)
        mine = odd * src_me + (1 - odd) * tgt_me
        return copy(vec.at[e, h], inbox.at[e, h, mine], e_send.at[e, h], e_recv.at[e, h], peer)

    def send_half(e, h):
        for k in range(1, NB):
            message(e, h, k).start()
        inbox[e, h, (e % 2) * src_me + (1 - e % 2) * tgt_me] = vec[e, h]

    def all_bytes(e, h, sem):
        others = inbox.at[e, h, pl.ds(0, NB - 1)]
        return pltpu.make_async_copy(others, others, sem.at[e, h])

    def receive(e):
        for h in range(2):
            all_bytes(e, h, e_recv).wait()
        pieces = [inbox[e, :, k].reshape(NB, B) for k in range(NB)]
        high = functools.reduce(jnp.maximum, pieces)
        level = high + jnp.log2(functools.reduce(jnp.add, [jnp.exp2(p - high) for p in pieces]))
        side = e % 2
        log = logmass[side] * LOG2E - level
        put_bias(bias.at[side], log * (1.0 / SCALE))
        dual[side] = log * (EPS / LOG2E) + norm[side]

    half_rows = pl.ds(pl.multiple_of(src_me % 2 * (N // 2), N // 2), N // 2)

    def spread(k):
        return copy(rows.at[1, half_rows, :], rows.at[1 + k, half_rows, :], x_send.at[k - 1], x_recv.at[k - 1], lo_peer("tgt", k))

    def hand_over(k):
        there = rows.at[1 + k, half_rows, :]
        return copy(there, there, f_send.at[k - 1], f_recv.at[k - 1], {"src": src_me + 1 - 2 * (src_me % 2)})

    def whole_pass(e, carry):
        receive(e - 1)

        @pl.when(e == 1)
        def _():
            for k in range(1, Q):
                spread(k).start()

        side = (e - 1) % 2

        def half(h, carry):
            def body(k, carry):
                at = h * (NB // 4) + k
                total = lse_tile(rows.at[side], bias.at[side], under(rows_t.at[1 - side], 2 * at, 2 * at + 1))
                vec[e, h, pl.ds(2 * k, 1), :] = total[:, :B]
                vec[e, h, pl.ds(2 * k + 1, 1), :] = total[:, B:]
                return carry

            lax.fori_loop(0, NB // 4, body, 0, unroll=UNROLL)
            send_half(e, h)
            return carry

        lax.fori_loop(0, 2, half, 0)

        @pl.when(e == 2)
        def _():
            for k in range(1, Q):
                spread(k).wait_recv()
                hand_over(k).start()

        return carry

    send_half(0, 0)
    send_half(0, 1)
    lax.fori_loop(1, 4, whole_pass, 0)
    for k in range(1, Q):
        hand_over(k).wait_recv()

    def turn_far(j, carry):
        for k in range(NB):
            rows_t[j, :, pl.ds(k * B, B)] = rows[j, pl.ds(k * B, B), :].astype(F32).T.astype(BF)
        return carry

    lax.fori_loop(2, 2 + Q - 1, turn_far, 0)
    receive(3)
    sd_ref[...] = dual[0]
    td_ref[...] = dual[1]

    def send_bias(k):
        return copy(far_bias.at[0], far_bias.at[k], b_send.at[k - 1], b_recv.at[k - 1], lo_peer("tgt", k))

    far_bias[0] = (dual[1] - tgt_norm[...]) * (LOG2E / (EPS * SCALE))
    for k in range(1, Q):
        send_bias(k).start()

    near = (t_hi, t_hi + 1 - 2 * (t_hi % 2), (t_hi + 2) % Q, Q - 1 - t_hi)

    def blocks_of(tile):
        first = tile * near[1] + (1 - tile) * near[2]
        second = tile * near[0] + (1 - tile) * near[3]
        return under(src_t, first * Q + t_lo, second * Q + t_lo)

    high[...] = jnp.full((2, 8, 2 * B), -1e30, F32)
    mass[...] = jnp.zeros((2, 8, 2 * B), F32)
    moment[...] = jnp.zeros((2, B, 2 * B), F32)

    def add_moments(tile, j):
        top, weight, total = moment_step(
            rows.at[j], rows_t.at[j], bias.at[j], blocks_of(tile), high[tile, pl.ds(0, 1), :], mass[tile], moment[tile]
        )
        high[tile] = jnp.broadcast_to(top, (8, 2 * B))
        mass[tile] = weight
        moment[tile] = total

    def own_moments(tile, carry):
        add_moments(tile, 1)
        return carry

    lax.fori_loop(0, 2, own_moments, 0)
    for k in range(1, Q):
        send_bias(k).wait_recv()
        put_bias(bias.at[1 + k], far_bias[k])

    def send_part(r):
        return copy(part.at[r], got.at[r - 1], r_send.at[r - 1], r_recv.at[r - 1], {"tgt": near[r] * Q + t_lo})

    def far_moments(tile, carry):
        def step(j, carry):
            add_moments(tile, j)
            return carry

        lax.fori_loop(2, 2 + Q - 1, step, 0)
        weight = jnp.sum(mass[tile], axis=0, keepdims=True)
        mean = moment[tile] / weight
        level = high[tile] * SCALE + jnp.log2(weight)
        for r, cut in ((2 - tile, pl.ds(0, B)), (3 - 3 * tile, pl.ds(B, B))):
            at = slice(cut.start, cut.start + B)
            part[r, pl.ds(0, B), :] = mean[:, at]
            part[r, pl.ds(B, 8), :] = level[:, at]

        @pl.when(tile == 0)
        def _():
            send_part(2).start()
            send_part(3).start()

        return carry

    lax.fori_loop(0, 2, far_moments, 0)
    send_part(1).start()

    def join(pieces):
        levels = [p[pl.ds(B, 8), :] for p in pieces]
        top = functools.reduce(jnp.maximum, levels)
        scaled = [jnp.exp2(v - top) for v in levels]
        total = functools.reduce(jnp.add, scaled)
        out = None
        for p, v in zip(pieces, scaled):
            term = p[pl.ds(0, B), :] * (v / total)[:1, :]
            out = term if out is None else out + term
        return out

    for r in range(1, Q):
        send_part(r).wait_recv()
    map_ref[...] = join([part.at[0]] + [got.at[j] for j in range(Q - 1)]).T

    for k in range(1, Q):
        gather_hi(k).wait_send()
        spread(k).wait_send()
        hand_over(k).wait_send()
        send_bias(k).wait_send()
        send_part(k).wait_send()
        for d in range(Q):
            gather_lo(d, k).wait_send()
    for e in range(4):
        for h in range(2):
            all_bytes(e, h, e_send).wait()


def shards(sources, targets, src_logmass, tgt_logmass):
    vmem = pl.BlockSpec(memory_space=pltpu.VMEM)
    dma = pltpu.SemaphoreType.DMA
    mapped, src_dual, tgt_dual = pl.pallas_call(
        kernel,
        out_shape=(
            jax.ShapeDtypeStruct((B, D), F32),
            jax.ShapeDtypeStruct((NB, B), F32),
            jax.ShapeDtypeStruct((NB, B), F32),
        ),
        in_specs=[pl.BlockSpec(memory_space=pltpu.HBM)] * 4,
        out_specs=(vmem, vmem, vmem),
        scratch_shapes=[
            pltpu.VMEM((1 + Q, N, D), BF),
            pltpu.VMEM((1 + Q, D, N), BF),
            pltpu.VMEM((1 + Q, N, B), BF),
            pltpu.VMEM((FILL, NB, B), F32),
            pltpu.VMEM((2, NB, B), F32),
            pltpu.VMEM((2, NB, B), F32),
            pltpu.VMEM((4, 2, NB // 2, B), F32),
            pltpu.VMEM((4, 2, NB, NB // 2, B), F32),
            pltpu.VMEM((2, B, 2 * B), F32),
            pltpu.VMEM((2, 8, 2 * B), F32),
            pltpu.VMEM((2, 8, 2 * B), F32),
            pltpu.VMEM((Q, NB, B), F32),
            pltpu.VMEM((Q, B + 8, D), F32),
            pltpu.VMEM((Q - 1, B + 8, D), F32),
            dma((4,)),
            dma((Q - 1,)), dma((Q - 1,)), dma((Q, Q - 1)), dma((Q, Q - 1)),
            dma((4, 2)), dma((4, 2)),
            *[dma((Q - 1,))] * 8,
        ],
        compiler_params=pltpu.CompilerParams(
            collective_id=0, has_side_effects=True, vmem_limit_bytes=64 * 1024 * 1024
        ),
    )(sources, targets, src_logmass.reshape(NB, B), tgt_logmass.reshape(NB, B))
    return mapped, src_dual.reshape(N), tgt_dual.reshape(N)


def solution(mesh):
    return jax.shard_map(
        shards,
        mesh=mesh,
        in_specs=(P(("src", "tgt"), None), P("tgt", None), P("src"), P("tgt")),
        out_specs=(P(("src", "tgt"), None), P("src"), P("tgt")),
        check_vma=False,
    )
```

```python
import functools
import math

import jax
import jax.numpy as jnp
from jax import lax
from jax.experimental import pallas as pl
from jax.experimental.pallas import tpu as pltpu
from jax.sharding import PartitionSpec as P

MESH = pl.DeviceIdType.MESH
EPS = 0.03125
LOG2E = math.log2(math.e)
B = 128
NB = 16
N = B * NB
D = 128
Q = 4
SCALE = LOG2E / (D * EPS)
BF = jnp.bfloat16
F32 = jnp.float32


FILL = 6860
GROUP = 16


def fold(x, op):
    x = op(x.reshape(x.shape[0] // GROUP, GROUP, x.shape[1]), axis=0)
    half = GROUP // 2
    return jnp.maximum(x[:half], x[half:]) if op is jnp.max else x[:half] + x[half:]


def lse_chunks(rows, bias, rhs, first, count, high, total):
    for q in range(count):
        at = pl.ds(pl.multiple_of((first + q) * B, B), B)
        u = jnp.dot(jnp.concatenate([rows[at, :], bias[at, :]], axis=1), rhs, preferred_element_type=F32)
        new = jnp.maximum(high, fold(u, jnp.max))
        part = jnp.exp2((u.reshape(B // 8, 8, u.shape[1]) - new[None]) * SCALE).reshape(u.shape)
        total = total * jnp.exp2((high - new) * SCALE) + fold(part, jnp.sum)
        high = new
    return high, total


def lse_end(high, total):
    y = high * SCALE + jnp.log2(total)
    top = jnp.max(y, axis=0, keepdims=True)
    return top + jnp.log2(jnp.sum(jnp.exp2(y - top), axis=0, keepdims=True))


def lse_tile(rows, bias, rhs):
    start = jnp.full((8, rhs.shape[1]), LOW, F32), jnp.zeros((8, rhs.shape[1]), F32)
    return lse_end(*lse_chunks(rows, bias, rhs, 0, NB, *start))


LOW = -1e30
HALF = NB // 2
CHUNK = 256
UNROLL = 4


def moment_step(rows, rows_t, bias, rhs, high, mass, total):
    for q in range(N // CHUNK):
        at = pl.ds(q * CHUNK, CHUNK)
        u = jnp.dot(jnp.concatenate([rows[at, :], bias[at, :]], axis=1), rhs, preferred_element_type=F32)
        new = jnp.maximum(high, jnp.max(fold(u, jnp.max), axis=0, keepdims=True))
        w = jnp.exp2((u - new) * SCALE)
        w_hi = w.astype(BF)
        w_lo = (w - w_hi.astype(F32)).astype(BF)
        lhs = rows_t[:, at]
        ratio = jnp.exp2((high - new) * SCALE)
        mass = mass * ratio + fold(w, jnp.sum)
        part = jnp.dot(lhs, w_hi, preferred_element_type=F32) + jnp.dot(lhs, w_lo, preferred_element_type=F32)
        total = total * ratio + part
        high = new
    return high, mass, total


def kernel(
    src_hbm, tgt_hbm, slm_hbm, tlm_hbm, map_ref, sd_ref, td_ref,
    rows, rows_t, bias, logmass, norm, dual, vec, inbox,
    run_high, run_total, moment, mass, high, far_bias, part, got, in_sem,
    g_hi_send, g_hi_recv, g_lo_send, g_lo_recv,
    e_send, e_recv, x_send, x_recv, f_send, f_recv, b_send, b_recv, r_send, r_recv,
):
    src_me = lax.axis_index("src")
    tgt_me = lax.axis_index("tgt")
    s_hi, s_lo = src_me // Q, src_me % Q
    t_hi, t_lo = tgt_me // Q, tgt_me % Q

    def lo_peer(axis, k):
        hi, lo = (s_hi, s_lo) if axis == "src" else (t_hi, t_lo)
        return {axis: hi * Q + (lo + k) % Q}

    def hi_peer(axis, k):
        hi, lo = (s_hi, s_lo) if axis == "src" else (t_hi, t_lo)
        return {axis: ((hi + k) % Q) * Q + lo}

    codes, src_t, src_norm = rows.at[0], rows_t.at[0], norm.at[0]
    tgt_ref, tgt_t, tgt_norm, tgt_bias = rows.at[1], rows_t.at[1], norm.at[1], bias.at[1]

    def block_at(k):
        return pl.ds(pl.multiple_of(k * B, B), B)

    fetches = [
        pltpu.make_async_copy(src, dst, in_sem.at[i])
        for i, (src, dst) in enumerate((
            (src_hbm, codes.at[block_at(tgt_me), :]), (tgt_hbm, tgt_ref), (slm_hbm, logmass.at[0]), (tlm_hbm, logmass.at[1]),
        ))
    ]
    for f in fetches:
        f.start()

    barrier = pltpu.get_barrier_semaphore()
    for k in range(1, NB):
        for axis, me in (("tgt", tgt_me), ("src", src_me)):
            pl.semaphore_signal(barrier, 1, device_id={axis: (me + k) % NB}, device_id_type=MESH)

    def copy(src, dst, send, recv, peer):
        return pltpu.make_async_remote_copy(
            src_ref=src, dst_ref=dst, send_sem=send, recv_sem=recv, device_id=peer, device_id_type=MESH
        )

    def gather_hi(k):
        own = codes.at[block_at(tgt_me), :]
        return copy(own, own, g_hi_send.at[k - 1], g_hi_recv.at[k - 1], hi_peer("tgt", k))

    def gather_lo(d, k):
        block = ((t_hi - d + Q) % Q) * Q + t_lo
        rows = codes.at[block_at(block), :]
        return copy(rows, rows, g_lo_send.at[d, k - 1], g_lo_recv.at[d, k - 1], lo_peer("tgt", k))

    lane = lax.broadcasted_iota(jnp.int32, (B, B), 1)
    ones = jnp.ones((D, 2 * B), BF)

    def put_bias(out, values, half):
        hi = values.astype(BF).astype(F32)
        rest = values - hi
        mid = rest.astype(BF).astype(F32)
        low = rest - mid
        turned = jnp.concatenate([hi, mid, low, jnp.zeros((B - 3 * HALF, B), F32)], axis=0).T
        for k in range(HALF):
            out[block_at(half * HALF + k), :] = jnp.where(lane % HALF == k, turned, 0.0).astype(BF)

    def turn(rows, rows_t, norm, at):
        turned = rows.astype(F32).T
        rows_t[:, block_at(at)] = turned.astype(BF)
        norm[pl.ds(at, 1), :] = jnp.sum(turned * turned, axis=0, keepdims=True) * (0.5 / D)

    def under(rows_t, first, second):
        pair = jnp.concatenate([rows_t[:, block_at(first)], rows_t[:, block_at(second)]], axis=1)
        return jnp.concatenate([pair, ones], axis=0)

    fetches[0].wait()
    pl.semaphore_wait(barrier, 2 * (NB - 1))
    for k in range(1, Q):
        gather_hi(k).start()
    for k in range(1, Q):
        gather_lo(0, k).start()

    for f in fetches[1:]:
        f.wait()
    for k in range(NB):
        turn(tgt_ref[pl.ds(k * B, B), :], tgt_t, tgt_norm, k)
    for half in range(2):
        put_bias(tgt_bias, tgt_norm[pl.ds(half * HALF, HALF), :] * (-LOG2E / (EPS * SCALE)), half)

    def take(at):
        turn(codes[block_at(at), :], src_t, src_norm, at)

    def first_pair(first, second):
        total = lse_tile(tgt_ref, tgt_bias, under(src_t, first, second))
        vec[0, first // 8, pl.ds(first % 8, 1), :] = total[:, :B]
        vec[0, second // 8, pl.ds(second % 8, 1), :] = total[:, B:]

    for d in range(1, Q):
        gather_hi(d).wait_recv()
        for k in range(1, Q):
            gather_lo(d, k).start()

    def first_group(d, carry):
        hi = (t_hi - d + Q) % Q
        at = [hi * Q + (t_lo - k + Q) % Q for k in range(Q)]
        take(at[0])
        gather_lo(d, 1).wait_recv()
        take(at[1])
        first_pair(at[0], at[1])
        gather_lo(d, 2).wait_recv()
        take(at[2])
        gather_lo(d, 3).wait_recv()
        take(at[3])
        first_pair(at[2], at[3])
        return carry

    lax.fori_loop(0, Q, first_group, 0)

    def message(e, h, k):
        odd = e % 2
        peer = ((src_me + odd * k) % NB, (tgt_me + (1 - odd) * k) % NB)
        mine = odd * src_me + (1 - odd) * tgt_me
        return copy(vec.at[e, h], inbox.at[e, h, mine], e_send.at[e, h], e_recv.at[e, h], peer)

    def send_half(e, h):
        for k in range(1, NB):
            message(e, h, k).start()
        inbox[e, h, (e % 2) * src_me + (1 - e % 2) * tgt_me] = vec[e, h]

    def all_bytes(e, h, sem):
        others = inbox.at[e, h, pl.ds(0, NB - 1)]
        return pltpu.make_async_copy(others, others, sem.at[e, h])

    def receive(e, h):
        all_bytes(e, h, e_recv).wait()
        pieces = [inbox[e, h, k] for k in range(NB)]
        top = functools.reduce(jnp.maximum, pieces)
        level = top + jnp.log2(functools.reduce(jnp.add, [jnp.exp2(p - top) for p in pieces]))
        side = e % 2
        here = pl.ds(pl.multiple_of(h * HALF, HALF), HALF)
        log = logmass[side, here, :] * LOG2E - level
        put_bias(bias.at[side], log * (1.0 / SCALE), h)
        dual[side, here, :] = log * (EPS / LOG2E) + norm[side, here, :]

    half_rows = pl.ds(pl.multiple_of(src_me % 2 * (N // 2), N // 2), N // 2)

    def spread(k):
        return copy(rows.at[1, half_rows, :], rows.at[1 + k, half_rows, :], x_send.at[k - 1], x_recv.at[k - 1], lo_peer("tgt", k))

    def hand_over(k):
        there = rows.at[1 + k, half_rows, :]
        return copy(there, there, f_send.at[k - 1], f_recv.at[k - 1], {"src": src_me + 1 - 2 * (src_me % 2)})

    def whole_pass(e, carry):
        side = (e - 1) % 2
        late = jnp.minimum(e - 1, 1)
        run_high[...] = jnp.full((8, N), LOW, F32)
        run_total[...] = jnp.zeros((8, N), F32)

        def quarter(s, carry):
            slow, fast = s // 2, s % 2
            h = late * fast + (1 - late) * slow
            m = late * slow + (1 - late) * fast

            @pl.when(s == 0)
            def _():
                receive(e - 1, 0)

            @pl.when(s == 2 * late)
            def _():
                receive(e - 1, 1)

            @pl.when((s == 0) & (e == 1))
            def _():
                for k in range(1, Q):
                    spread(k).start()

            def body(k, carry):
                at = h * (HALF // 2) + k
                here = pl.ds(pl.multiple_of(at * 2 * B, 2 * B), 2 * B)
                rhs = under(rows_t.at[1 - side], 2 * at, 2 * at + 1)
                run_high[:, here], run_total[:, here] = lse_chunks(
                    rows.at[side], bias.at[side], rhs, m * HALF, HALF, run_high[:, here], run_total[:, here]
                )
                return carry

            lax.fori_loop(0, HALF // 2, body, 0, unroll=UNROLL)

            @pl.when(m == 1)
            def _():
                here = pl.ds(pl.multiple_of(h * (N // 2), N // 2), N // 2)
                out = lse_end(run_high[:, here], run_total[:, here])
                for k in range(HALF):
                    vec[e, h, pl.ds(k, 1), :] = out[:, k * B : (k + 1) * B]
                send_half(e, h)

            return carry

        lax.fori_loop(0, 4, quarter, 0)

        @pl.when(e == 2)
        def _():
            for k in range(1, Q):
                spread(k).wait_recv()
                hand_over(k).start()

        return carry

    send_half(0, 0)
    send_half(0, 1)
    lax.fori_loop(1, 4, whole_pass, 0)
    for k in range(1, Q):
        hand_over(k).wait_recv()

    def turn_far(j, carry):
        for k in range(NB):
            rows_t[j, :, pl.ds(k * B, B)] = rows[j, pl.ds(k * B, B), :].astype(F32).T.astype(BF)
        return carry

    lax.fori_loop(2, 2 + Q - 1, turn_far, 0)
    receive(3, 0)
    receive(3, 1)
    sd_ref[...] = dual[0]
    td_ref[...] = dual[1]

    def send_bias(k):
        return copy(far_bias.at[0], far_bias.at[k], b_send.at[k - 1], b_recv.at[k - 1], lo_peer("tgt", k))

    far_bias[0] = (dual[1] - tgt_norm[...]) * (LOG2E / (EPS * SCALE))
    for k in range(1, Q):
        send_bias(k).start()

    near = (t_hi, t_hi + 1 - 2 * (t_hi % 2), (t_hi + 2) % Q, Q - 1 - t_hi)

    def blocks_of(tile):
        first = tile * near[1] + (1 - tile) * near[2]
        second = tile * near[0] + (1 - tile) * near[3]
        return under(src_t, first * Q + t_lo, second * Q + t_lo)

    high[...] = jnp.full((2, 8, 2 * B), LOW, F32)
    mass[...] = jnp.zeros((2, 8, 2 * B), F32)
    moment[...] = jnp.zeros((2, B, 2 * B), F32)

    def add_moments(tile, j):
        top, weight, total = moment_step(
            rows.at[j], rows_t.at[j], bias.at[j], blocks_of(tile), high[tile, pl.ds(0, 1), :], mass[tile], moment[tile]
        )
        high[tile] = jnp.broadcast_to(top, (8, 2 * B))
        mass[tile] = weight
        moment[tile] = total

    def own_moments(tile, carry):
        add_moments(tile, 1)
        return carry

    lax.fori_loop(0, 2, own_moments, 0)
    for k in range(1, Q):
        send_bias(k).wait_recv()
        for half in range(2):
            put_bias(bias.at[1 + k], far_bias[k, pl.ds(half * HALF, HALF), :], half)

    def send_part(r):
        return copy(part.at[r], got.at[r - 1], r_send.at[r - 1], r_recv.at[r - 1], {"tgt": near[r] * Q + t_lo})

    def far_moments(tile, carry):
        def step(j, carry):
            add_moments(tile, j)
            return carry

        lax.fori_loop(2, 2 + Q - 1, step, 0)
        weight = jnp.sum(mass[tile], axis=0, keepdims=True)
        mean = moment[tile] / weight
        level = high[tile] * SCALE + jnp.log2(weight)
        for r, cut in ((2 - tile, pl.ds(0, B)), (3 - 3 * tile, pl.ds(B, B))):
            at = slice(cut.start, cut.start + B)
            part[r, pl.ds(0, B), :] = mean[:, at]
            part[r, pl.ds(B, 8), :] = level[:, at]

        @pl.when(tile == 0)
        def _():
            send_part(2).start()
            send_part(3).start()

        return carry

    lax.fori_loop(0, 2, far_moments, 0)
    send_part(1).start()

    def join(pieces):
        levels = [p[pl.ds(B, 8), :] for p in pieces]
        top = functools.reduce(jnp.maximum, levels)
        scaled = [jnp.exp2(v - top) for v in levels]
        total = functools.reduce(jnp.add, scaled)
        out = None
        for p, v in zip(pieces, scaled):
            term = p[pl.ds(0, B), :] * (v / total)[:1, :]
            out = term if out is None else out + term
        return out

    for r in range(1, Q):
        send_part(r).wait_recv()
    map_ref[...] = join([part.at[0]] + [got.at[j] for j in range(Q - 1)]).T

    for k in range(1, Q):
        gather_hi(k).wait_send()
        spread(k).wait_send()
        hand_over(k).wait_send()
        send_bias(k).wait_send()
        send_part(k).wait_send()
        for d in range(Q):
            gather_lo(d, k).wait_send()
    for e in range(4):
        for h in range(2):
            all_bytes(e, h, e_send).wait()


def hand_on(mapped, src_dual, tgt_dual, mapped_out, src_out, tgt_out):
    mapped_out[...] = mapped[...]
    src_out[...] = src_dual[...]
    tgt_out[...] = tgt_dual[...]


def shards(sources, targets, src_logmass, tgt_logmass):
    vmem = pl.BlockSpec(memory_space=pltpu.VMEM)
    dma = pltpu.SemaphoreType.DMA
    results = (
        jax.ShapeDtypeStruct((B, D), F32),
        jax.ShapeDtypeStruct((NB, B), F32),
        jax.ShapeDtypeStruct((NB, B), F32),
    )
    found = pl.pallas_call(
        kernel,
        out_shape=results,
        in_specs=[pl.BlockSpec(memory_space=pltpu.HBM)] * 4,
        out_specs=(vmem, vmem, vmem),
        scratch_shapes=[
            pltpu.VMEM((1 + Q, N, D), BF),
            pltpu.VMEM((1 + Q, D, N), BF),
            pltpu.VMEM((1 + Q, N, B), BF),
            pltpu.VMEM((FILL, NB, B), F32),
            pltpu.VMEM((2, NB, B), F32),
            pltpu.VMEM((2, NB, B), F32),
            pltpu.VMEM((4, 2, NB // 2, B), F32),
            pltpu.VMEM((4, 2, NB, NB // 2, B), F32),
            pltpu.VMEM((8, N), F32),
            pltpu.VMEM((8, N), F32),
            pltpu.VMEM((2, B, 2 * B), F32),
            pltpu.VMEM((2, 8, 2 * B), F32),
            pltpu.VMEM((2, 8, 2 * B), F32),
            pltpu.VMEM((Q, NB, B), F32),
            pltpu.VMEM((Q, B + 8, D), F32),
            pltpu.VMEM((Q - 1, B + 8, D), F32),
            dma((4,)),
            dma((Q - 1,)), dma((Q - 1,)), dma((Q, Q - 1)), dma((Q, Q - 1)),
            dma((4, 2)), dma((4, 2)),
            *[dma((Q - 1,))] * 8,
        ],
        compiler_params=pltpu.CompilerParams(
            collective_id=0, has_side_effects=True, vmem_limit_bytes=64 * 1024 * 1024
        ),
    )(sources, targets, src_logmass.reshape(NB, B), tgt_logmass.reshape(NB, B))
    mapped, src_dual, tgt_dual = pl.pallas_call(
        hand_on,
        out_shape=results,
        in_specs=[vmem] * 3,
        out_specs=(vmem,) * 3,
    )(*found)
    return mapped, src_dual.reshape(N), tgt_dual.reshape(N)


def solution(mesh):
    return jax.shard_map(
        shards,
        mesh=mesh,
        in_specs=(P(("src", "tgt"), None), P("tgt", None), P("src"), P("tgt")),
        out_specs=(P(("src", "tgt"), None), P("src"), P("tgt")),
        check_vma=False,
    )
```

```python
import functools
import math

import jax
import jax.numpy as jnp
from jax import lax
from jax.experimental import pallas as pl
from jax.experimental.pallas import tpu as pltpu
from jax.sharding import PartitionSpec as P

MESH = pl.DeviceIdType.MESH
EPS = 0.03125
LOG2E = math.log2(math.e)
B = 128
NB = 16
N = B * NB
D = 128
Q = 4
SCALE = LOG2E / (D * EPS)
BF = jnp.bfloat16
F32 = jnp.float32


FILL = 6860
GROUP = 16


def fold(x, op):
    x = op(x.reshape(x.shape[0] // GROUP, GROUP, x.shape[1]), axis=0)
    half = GROUP // 2
    return jnp.maximum(x[:half], x[half:]) if op is jnp.max else x[:half] + x[half:]


def lse_chunks(rows, bias, rhs, first, count, high, total):
    for q in range(count):
        at = pl.ds(pl.multiple_of((first + q) * B, B), B)
        u = jnp.dot(jnp.concatenate([rows[at, :], bias[at, :]], axis=1), rhs, preferred_element_type=F32)
        new = jnp.maximum(high, fold(u, jnp.max))
        part = jnp.exp2((u.reshape(B // 8, 8, u.shape[1]) - new[None]) * SCALE).reshape(u.shape)
        total = total * jnp.exp2((high - new) * SCALE) + fold(part, jnp.sum)
        high = new
    return high, total


def lse_end(high, total):
    y = high * SCALE + jnp.log2(total)
    top = jnp.max(y, axis=0, keepdims=True)
    return top + jnp.log2(jnp.sum(jnp.exp2(y - top), axis=0, keepdims=True))


def lse_tile(rows, bias, rhs):
    start = jnp.full((8, rhs.shape[1]), LOW, F32), jnp.zeros((8, rhs.shape[1]), F32)
    return lse_end(*lse_chunks(rows, bias, rhs, 0, NB, *start))


LOW = -1e30
HALF = NB // 2
CHUNK = 256
UNROLL = 4


def moment_step(rows, rows_t, bias, rhs, high, mass, total):
    for q in range(N // CHUNK):
        at = pl.ds(q * CHUNK, CHUNK)
        u = jnp.dot(jnp.concatenate([rows[at, :], bias[at, :]], axis=1), rhs, preferred_element_type=F32)
        new = jnp.maximum(high, jnp.max(fold(u, jnp.max), axis=0, keepdims=True))
        w = jnp.exp2((u - new) * SCALE)
        w_hi = w.astype(BF)
        w_lo = (w - w_hi.astype(F32)).astype(BF)
        lhs = rows_t[:, at]
        ratio = jnp.exp2((high - new) * SCALE)
        mass = mass * ratio + fold(w, jnp.sum)
        part = jnp.dot(lhs, w_hi, preferred_element_type=F32) + jnp.dot(lhs, w_lo, preferred_element_type=F32)
        total = total * ratio + part
        high = new
    return high, mass, total


def kernel(
    src_hbm, tgt_hbm, slm_hbm, tlm_hbm, map_ref, sd_ref, td_ref,
    rows, rows_t, bias, logmass, norm, dual, vec, inbox,
    run_high, run_total, moment, mass, high, far_bias, part, got, in_sem,
    g_hi_send, g_hi_recv, g_lo_send, g_lo_recv,
    e_send, e_recv, x_send, x_recv, f_send, f_recv, b_send, b_recv, r_send, r_recv,
):
    src_me = lax.axis_index("src")
    tgt_me = lax.axis_index("tgt")
    s_hi, s_lo = src_me // Q, src_me % Q
    t_hi, t_lo = tgt_me // Q, tgt_me % Q

    def lo_peer(axis, k):
        hi, lo = (s_hi, s_lo) if axis == "src" else (t_hi, t_lo)
        return {axis: hi * Q + (lo + k) % Q}

    def hi_peer(axis, k):
        hi, lo = (s_hi, s_lo) if axis == "src" else (t_hi, t_lo)
        return {axis: ((hi + k) % Q) * Q + lo}

    codes, src_t, src_norm = rows.at[0], rows_t.at[0], norm.at[0]
    tgt_ref, tgt_t, tgt_norm, tgt_bias = rows.at[1], rows_t.at[1], norm.at[1], bias.at[1]

    def block_at(k):
        return pl.ds(pl.multiple_of(k * B, B), B)

    fetches = [
        pltpu.make_async_copy(src, dst, in_sem.at[i])
        for i, (src, dst) in enumerate((
            (src_hbm, codes.at[block_at(tgt_me), :]), (tgt_hbm, tgt_ref), (slm_hbm, logmass.at[0]), (tlm_hbm, logmass.at[1]),
        ))
    ]
    for f in fetches:
        f.start()

    barrier = pltpu.get_barrier_semaphore()
    for k in range(1, Q):
        pl.semaphore_signal(barrier, 1, device_id=lo_peer("tgt", k), device_id_type=MESH)
        pl.semaphore_signal(barrier, 1, device_id=hi_peer("tgt", k), device_id_type=MESH)
    side, core = s_lo // 2, s_lo % 2
    edge = (Q - 1) * (1 - t_hi // 2)
    for k in range(Q):
        for c in range(2):
            row, other = ((s_hi + k) % Q) * Q, (core + c) % 2
            if k or c:
                pl.semaphore_signal(
                    barrier, 1, device_id=(row + side * 2 + other, tgt_me), device_id_type=MESH
                )
            pl.semaphore_signal(
                barrier, 1, device_id=(row + (1 - side) * 2 + other, edge * Q + t_lo), device_id_type=MESH
            )
    greeted = 2 * (Q - 1) + 2 * Q - 1 + 4 * Q * (1 - (t_hi + 1) // 2 % 2)

    def copy(src, dst, send, recv, peer):
        return pltpu.make_async_remote_copy(
            src_ref=src, dst_ref=dst, send_sem=send, recv_sem=recv, device_id=peer, device_id_type=MESH
        )

    def gather_hi(k):
        own = codes.at[block_at(tgt_me), :]
        return copy(own, own, g_hi_send.at[k - 1], g_hi_recv.at[k - 1], hi_peer("tgt", k))

    def gather_lo(d, k):
        block = ((t_hi - d + Q) % Q) * Q + t_lo
        rows = codes.at[block_at(block), :]
        return copy(rows, rows, g_lo_send.at[d, k - 1], g_lo_recv.at[d, k - 1], lo_peer("tgt", k))

    lane = lax.broadcasted_iota(jnp.int32, (B, B), 1)
    ones = jnp.ones((D, 2 * B), BF)

    def put_bias(out, values, half):
        hi = values.astype(BF).astype(F32)
        rest = values - hi
        mid = rest.astype(BF).astype(F32)
        low = rest - mid
        turned = jnp.concatenate([hi, mid, low, jnp.zeros((B - 3 * HALF, B), F32)], axis=0).T
        for k in range(HALF):
            out[block_at(half * HALF + k), :] = jnp.where(lane % HALF == k, turned, 0.0).astype(BF)

    def turn(rows, rows_t, norm, at):
        turned = rows.astype(F32).T
        rows_t[:, block_at(at)] = turned.astype(BF)
        norm[pl.ds(at, 1), :] = jnp.sum(turned * turned, axis=0, keepdims=True) * (0.5 / D)

    def under(rows_t, first, second):
        pair = jnp.concatenate([rows_t[:, block_at(first)], rows_t[:, block_at(second)]], axis=1)
        return jnp.concatenate([pair, ones], axis=0)

    fetches[0].wait()
    pl.semaphore_wait(barrier, greeted)
    for k in range(1, Q):
        gather_hi(k).start()
    for k in range(1, Q):
        gather_lo(0, k).start()

    for f in fetches[1:]:
        f.wait()
    for k in range(NB):
        turn(tgt_ref[pl.ds(k * B, B), :], tgt_t, tgt_norm, k)
    for half in range(2):
        put_bias(tgt_bias, tgt_norm[pl.ds(half * HALF, HALF), :] * (-LOG2E / (EPS * SCALE)), half)

    def take(at):
        turn(codes[block_at(at), :], src_t, src_norm, at)

    def first_pair(first, second):
        total = lse_tile(tgt_ref, tgt_bias, under(src_t, first, second))
        vec[0, first // 8, pl.ds(first % 8, 1), :] = total[:, :B]
        vec[0, second // 8, pl.ds(second % 8, 1), :] = total[:, B:]

    for d in range(1, Q):
        gather_hi(d).wait_recv()
        for k in range(1, Q):
            gather_lo(d, k).start()

    def first_group(d, carry):
        hi = (t_hi - d + Q) % Q
        at = [hi * Q + (t_lo - k + Q) % Q for k in range(Q)]
        take(at[0])
        gather_lo(d, 1).wait_recv()
        take(at[1])
        first_pair(at[0], at[1])
        gather_lo(d, 2).wait_recv()
        take(at[2])
        gather_lo(d, 3).wait_recv()
        take(at[3])
        first_pair(at[2], at[3])
        return carry

    lax.fori_loop(0, Q, first_group, 0)

    def message(e, h, k):
        odd = e % 2
        peer = ((src_me + odd * k) % NB, (tgt_me + (1 - odd) * k) % NB)
        mine = odd * src_me + (1 - odd) * tgt_me
        return copy(vec.at[e, h], inbox.at[e, h, mine], e_send.at[e, h], e_recv.at[e, h], peer)

    def send_half(e, h):
        for k in range(1, NB):
            message(e, h, k).start()
        inbox[e, h, (e % 2) * src_me + (1 - e % 2) * tgt_me] = vec[e, h]

    def all_bytes(e, h, sem):
        others = inbox.at[e, h, pl.ds(0, NB - 1)]
        return pltpu.make_async_copy(others, others, sem.at[e, h])

    def receive(e, h):
        all_bytes(e, h, e_recv).wait()
        pieces = [inbox[e, h, k] for k in range(NB)]
        top = functools.reduce(jnp.maximum, pieces)
        level = top + jnp.log2(functools.reduce(jnp.add, [jnp.exp2(p - top) for p in pieces]))
        side = e % 2
        here = pl.ds(pl.multiple_of(h * HALF, HALF), HALF)
        log = logmass[side, here, :] * LOG2E - level
        put_bias(bias.at[side], log * (1.0 / SCALE), h)
        dual[side, here, :] = log * (EPS / LOG2E) + norm[side, here, :]

    half_rows = pl.ds(pl.multiple_of(src_me % 2 * (N // 2), N // 2), N // 2)

    def spread(k):
        return copy(rows.at[1, half_rows, :], rows.at[1 + k, half_rows, :], x_send.at[k - 1], x_recv.at[k - 1], lo_peer("tgt", k))

    def hand_over(k):
        there = rows.at[1 + k, half_rows, :]
        return copy(there, there, f_send.at[k - 1], f_recv.at[k - 1], {"src": src_me + 1 - 2 * (src_me % 2)})

    def whole_pass(e, carry):
        side = (e - 1) % 2
        late = jnp.minimum(e - 1, 1)
        run_high[...] = jnp.full((8, N), LOW, F32)
        run_total[...] = jnp.zeros((8, N), F32)

        def quarter(s, carry):
            slow, fast = s // 2, s % 2
            h = late * fast + (1 - late) * slow
            m = late * slow + (1 - late) * fast

            @pl.when(s == 0)
            def _():
                receive(e - 1, 0)

            @pl.when(s == 2 * late)
            def _():
                receive(e - 1, 1)

            @pl.when((s == 0) & (e == 1))
            def _():
                for k in range(1, Q):
                    spread(k).start()

            def body(k, carry):
                at = h * (HALF // 2) + k
                here = pl.ds(pl.multiple_of(at * 2 * B, 2 * B), 2 * B)
                rhs = under(rows_t.at[1 - side], 2 * at, 2 * at + 1)
                run_high[:, here], run_total[:, here] = lse_chunks(
                    rows.at[side], bias.at[side], rhs, m * HALF, HALF, run_high[:, here], run_total[:, here]
                )
                return carry

            lax.fori_loop(0, HALF // 2, body, 0, unroll=UNROLL)

            @pl.when(m == 1)
            def _():
                here = pl.ds(pl.multiple_of(h * (N // 2), N // 2), N // 2)
                out = lse_end(run_high[:, here], run_total[:, here])
                for k in range(HALF):
                    vec[e, h, pl.ds(k, 1), :] = out[:, k * B : (k + 1) * B]
                send_half(e, h)

            return carry

        lax.fori_loop(0, 4, quarter, 0)

        @pl.when(e == 2)
        def _():
            for k in range(1, Q):
                spread(k).wait_recv()
                hand_over(k).start()

        return carry

    send_half(0, 0)
    send_half(0, 1)
    lax.fori_loop(1, 4, whole_pass, 0)
    for k in range(1, Q):
        hand_over(k).wait_recv()

    def turn_far(j, carry):
        for k in range(NB):
            rows_t[j, :, pl.ds(k * B, B)] = rows[j, pl.ds(k * B, B), :].astype(F32).T.astype(BF)
        return carry

    lax.fori_loop(2, 2 + Q - 1, turn_far, 0)
    receive(3, 0)
    receive(3, 1)
    sd_ref[...] = dual[0]
    td_ref[...] = dual[1]

    def send_bias(k):
        return copy(far_bias.at[0], far_bias.at[k], b_send.at[k - 1], b_recv.at[k - 1], lo_peer("tgt", k))

    far_bias[0] = (dual[1] - tgt_norm[...]) * (LOG2E / (EPS * SCALE))
    for k in range(1, Q):
        send_bias(k).start()

    near = (t_hi, t_hi + 1 - 2 * (t_hi % 2), (t_hi + 2) % Q, Q - 1 - t_hi)

    def blocks_of(tile):
        first = tile * near[1] + (1 - tile) * near[2]
        second = tile * near[0] + (1 - tile) * near[3]
        return under(src_t, first * Q + t_lo, second * Q + t_lo)

    high[...] = jnp.full((2, 8, 2 * B), LOW, F32)
    mass[...] = jnp.zeros((2, 8, 2 * B), F32)
    moment[...] = jnp.zeros((2, B, 2 * B), F32)

    def add_moments(tile, j):
        top, weight, total = moment_step(
            rows.at[j], rows_t.at[j], bias.at[j], blocks_of(tile), high[tile, pl.ds(0, 1), :], mass[tile], moment[tile]
        )
        high[tile] = jnp.broadcast_to(top, (8, 2 * B))
        mass[tile] = weight
        moment[tile] = total

    def own_moments(tile, carry):
        add_moments(tile, 1)
        return carry

    lax.fori_loop(0, 2, own_moments, 0)
    for k in range(1, Q):
        send_bias(k).wait_recv()
        for half in range(2):
            put_bias(bias.at[1 + k], far_bias[k, pl.ds(half * HALF, HALF), :], half)

    def send_part(r):
        return copy(part.at[r], got.at[r - 1], r_send.at[r - 1], r_recv.at[r - 1], {"tgt": near[r] * Q + t_lo})

    def far_moments(tile, carry):
        def step(j, carry):
            add_moments(tile, j)
            return carry

        lax.fori_loop(2, 2 + Q - 1, step, 0)
        weight = jnp.sum(mass[tile], axis=0, keepdims=True)
        mean = moment[tile] / weight
        level = high[tile] * SCALE + jnp.log2(weight)
        for r, cut in ((2 - tile, pl.ds(0, B)), (3 - 3 * tile, pl.ds(B, B))):
            at = slice(cut.start, cut.start + B)
            part[r, pl.ds(0, B), :] = mean[:, at]
            part[r, pl.ds(B, 8), :] = level[:, at]

        @pl.when(tile == 0)
        def _():
            send_part(2).start()
            send_part(3).start()

        return carry

    lax.fori_loop(0, 2, far_moments, 0)
    send_part(1).start()

    def join(pieces):
        levels = [p[pl.ds(B, 8), :] for p in pieces]
        top = functools.reduce(jnp.maximum, levels)
        scaled = [jnp.exp2(v - top) for v in levels]
        total = functools.reduce(jnp.add, scaled)
        out = None
        for p, v in zip(pieces, scaled):
            term = p[pl.ds(0, B), :] * (v / total)[:1, :]
            out = term if out is None else out + term
        return out

    for r in range(1, Q):
        send_part(r).wait_recv()
    map_ref[...] = join([part.at[0]] + [got.at[j] for j in range(Q - 1)]).T

    for k in range(1, Q):
        gather_hi(k).wait_send()
        spread(k).wait_send()
        hand_over(k).wait_send()
        send_bias(k).wait_send()
        send_part(k).wait_send()
        for d in range(Q):
            gather_lo(d, k).wait_send()
    for e in range(4):
        for h in range(2):
            all_bytes(e, h, e_send).wait()


def hand_on(mapped, src_dual, tgt_dual, mapped_out, src_out, tgt_out):
    mapped_out[...] = mapped[...]
    src_out[...] = src_dual[...]
    tgt_out[...] = tgt_dual[...]


def shards(sources, targets, src_logmass, tgt_logmass):
    vmem = pl.BlockSpec(memory_space=pltpu.VMEM)
    dma = pltpu.SemaphoreType.DMA
    results = (
        jax.ShapeDtypeStruct((B, D), F32),
        jax.ShapeDtypeStruct((NB, B), F32),
        jax.ShapeDtypeStruct((NB, B), F32),
    )
    found = pl.pallas_call(
        kernel,
        out_shape=results,
        in_specs=[pl.BlockSpec(memory_space=pltpu.HBM)] * 4,
        out_specs=(vmem, vmem, vmem),
        scratch_shapes=[
            pltpu.VMEM((1 + Q, N, D), BF),
            pltpu.VMEM((1 + Q, D, N), BF),
            pltpu.VMEM((1 + Q, N, B), BF),
            pltpu.VMEM((FILL, NB, B), F32),
            pltpu.VMEM((2, NB, B), F32),
            pltpu.VMEM((2, NB, B), F32),
            pltpu.VMEM((4, 2, NB // 2, B), F32),
            pltpu.VMEM((4, 2, NB, NB // 2, B), F32),
            pltpu.VMEM((8, N), F32),
            pltpu.VMEM((8, N), F32),
            pltpu.VMEM((2, B, 2 * B), F32),
            pltpu.VMEM((2, 8, 2 * B), F32),
            pltpu.VMEM((2, 8, 2 * B), F32),
            pltpu.VMEM((Q, NB, B), F32),
            pltpu.VMEM((Q, B + 8, D), F32),
            pltpu.VMEM((Q - 1, B + 8, D), F32),
            dma((4,)),
            dma((Q - 1,)), dma((Q - 1,)), dma((Q, Q - 1)), dma((Q, Q - 1)),
            dma((4, 2)), dma((4, 2)),
            *[dma((Q - 1,))] * 8,
        ],
        compiler_params=pltpu.CompilerParams(
            collective_id=0, has_side_effects=True, vmem_limit_bytes=64 * 1024 * 1024
        ),
    )(sources, targets, src_logmass.reshape(NB, B), tgt_logmass.reshape(NB, B))
    mapped, src_dual, tgt_dual = pl.pallas_call(
        hand_on,
        out_shape=results,
        in_specs=[vmem] * 3,
        out_specs=(vmem,) * 3,
    )(*found)
    return mapped, src_dual.reshape(N), tgt_dual.reshape(N)


def solution(mesh):
    return jax.shard_map(
        shards,
        mesh=mesh,
        in_specs=(P(("src", "tgt"), None), P("tgt", None), P("src"), P("tgt")),
        out_specs=(P(("src", "tgt"), None), P("src"), P("tgt")),
        check_vma=False,
    )
```

```python
import functools
import math

import jax
import jax.numpy as jnp
from jax import lax
from jax.experimental import pallas as pl
from jax.experimental.pallas import tpu as pltpu
from jax.sharding import PartitionSpec as P

MESH = pl.DeviceIdType.MESH
EPS = 0.03125
LOG2E = math.log2(math.e)
B = 128
NB = 16
N = B * NB
D = 128
Q = 4
SCALE = LOG2E / (D * EPS)
BF = jnp.bfloat16
F32 = jnp.float32


FILL = 6860
GROUP = 16


def fold(x, op):
    x = op(x.reshape(x.shape[0] // GROUP, GROUP, x.shape[1]), axis=0)
    half = GROUP // 2
    return jnp.maximum(x[:half], x[half:]) if op is jnp.max else x[:half] + x[half:]


def lse_chunks(rows, bias, rhs, first, count, high, total):
    for q in range(count):
        at = pl.ds(pl.multiple_of((first + q) * B, B), B)
        u = jnp.dot(jnp.concatenate([rows[at, :], bias[at, :]], axis=1), rhs, preferred_element_type=F32)
        new = jnp.maximum(high, fold(u, jnp.max))
        part = jnp.exp2((u.reshape(B // 8, 8, u.shape[1]) - new[None]) * SCALE).reshape(u.shape)
        total = total * jnp.exp2((high - new) * SCALE) + fold(part, jnp.sum)
        high = new
    return high, total


def lse_end(high, total):
    y = high * SCALE + jnp.log2(total)
    top = jnp.max(y, axis=0, keepdims=True)
    return top + jnp.log2(jnp.sum(jnp.exp2(y - top), axis=0, keepdims=True))


def lse_tile(rows, bias, rhs):
    start = jnp.full((8, rhs.shape[1]), LOW, F32), jnp.zeros((8, rhs.shape[1]), F32)
    return lse_end(*lse_chunks(rows, bias, rhs, 0, NB, *start))


LOW = -1e30
HALF = NB // 2
CHUNK = 256
UNROLL = 4


def moment_step(rows, rows_t, bias, rhs, high, mass, total):
    for q in range(N // CHUNK):
        at = pl.ds(q * CHUNK, CHUNK)
        u = jnp.dot(jnp.concatenate([rows[at, :], bias[at, :]], axis=1), rhs, preferred_element_type=F32)
        new = jnp.maximum(high, jnp.max(fold(u, jnp.max), axis=0, keepdims=True))
        w = jnp.exp2((u - new) * SCALE)
        w_hi = w.astype(BF)
        w_lo = (w - w_hi.astype(F32)).astype(BF)
        lhs = rows_t[:, at]
        ratio = jnp.exp2((high - new) * SCALE)
        mass = mass * ratio + fold(w, jnp.sum)
        part = jnp.dot(lhs, w_hi, preferred_element_type=F32) + jnp.dot(lhs, w_lo, preferred_element_type=F32)
        total = total * ratio + part
        high = new
    return high, mass, total


def kernel(
    src_hbm, tgt_hbm, slm_hbm, tlm_hbm, map_ref, sd_ref, td_ref,
    rows, rows_t, bias, logmass, norm, dual, vec, inbox,
    run_high, run_total, moment, mass, high, far_bias, part, got, in_sem, here_sem,
    g_hi_send, g_hi_recv, g_lo_send, g_lo_recv,
    e_send, e_recv, x_send, x_recv, f_send, f_recv, b_send, b_recv, r_send, r_recv,
):
    src_me = lax.axis_index("src")
    tgt_me = lax.axis_index("tgt")
    s_hi, s_lo = src_me // Q, src_me % Q
    t_hi, t_lo = tgt_me // Q, tgt_me % Q

    def lo_peer(axis, k):
        hi, lo = (s_hi, s_lo) if axis == "src" else (t_hi, t_lo)
        return {axis: hi * Q + (lo + k) % Q}

    def hi_peer(axis, k):
        hi, lo = (s_hi, s_lo) if axis == "src" else (t_hi, t_lo)
        return {axis: ((hi + k) % Q) * Q + lo}

    codes, src_t, src_norm = rows.at[0], rows_t.at[0], norm.at[0]
    tgt_ref, tgt_t, tgt_norm, tgt_bias = rows.at[1], rows_t.at[1], norm.at[1], bias.at[1]

    def block_at(k):
        return pl.ds(pl.multiple_of(k * B, B), B)

    fetches = [
        pltpu.make_async_copy(src, dst, in_sem.at[i])
        for i, (src, dst) in enumerate((
            (src_hbm, codes.at[block_at(tgt_me), :]), (tgt_hbm, tgt_ref), (slm_hbm, logmass.at[0]), (tlm_hbm, logmass.at[1]),
        ))
    ]
    for f in fetches:
        f.start()

    barrier = pltpu.get_barrier_semaphore()
    side, core = s_lo // 2, s_lo % 2
    is_edge = t_hi == (Q - 1) * (1 - side)
    near_src = [
        {"src": ((s_hi + k) % Q) * Q + side * 2 + (core + c) % 2} for k in range(Q) for c in range(2) if k or c
    ]
    across = (s_hi * Q + (1 - side) * 2 + core, (Q - 1 - t_hi) * Q + t_lo)
    hi_peers = [hi_peer("tgt", k) for k in range(1, Q)]

    def signal_all(sem, peers):
        for peer in peers:
            pl.semaphore_signal(sem, 1, device_id=peer, device_id_type=MESH)

    signal_all(barrier, hi_peers + [lo_peer("tgt", k) for k in range(1, Q)] + near_src)

    @pl.when(is_edge)
    def _():
        signal_all(barrier, [across])

    greeted = 2 * (Q - 1) + len(near_src) + 1 - jnp.minimum(jnp.abs(t_hi - (Q - 1) * (1 - side)), 1)

    def copy(src, dst, send, recv, peer):
        return pltpu.make_async_remote_copy(
            src_ref=src, dst_ref=dst, send_sem=send, recv_sem=recv, device_id=peer, device_id_type=MESH
        )

    def gather_hi(k):
        own = codes.at[block_at(tgt_me), :]
        return copy(own, own, g_hi_send.at[k - 1], g_hi_recv.at[k - 1], hi_peer("tgt", k))

    def gather_lo(d, k):
        block = ((t_hi - d + Q) % Q) * Q + t_lo
        rows = codes.at[block_at(block), :]
        return copy(rows, rows, g_lo_send.at[d, k - 1], g_lo_recv.at[d, k - 1], lo_peer("tgt", k))

    lane = lax.broadcasted_iota(jnp.int32, (B, B), 1)
    ones = jnp.ones((D, 2 * B), BF)

    def put_bias(out, values, half):
        hi = values.astype(BF).astype(F32)
        rest = values - hi
        mid = rest.astype(BF).astype(F32)
        low = rest - mid
        turned = jnp.concatenate([hi, mid, low, jnp.zeros((B - 3 * HALF, B), F32)], axis=0).T
        for k in range(HALF):
            out[block_at(half * HALF + k), :] = jnp.where(lane % HALF == k, turned, 0.0).astype(BF)

    def turn(rows, rows_t, norm, at):
        turned = rows.astype(F32).T
        rows_t[:, block_at(at)] = turned.astype(BF)
        norm[pl.ds(at, 1), :] = jnp.sum(turned * turned, axis=0, keepdims=True) * (0.5 / D)

    def under(rows_t, first, second):
        pair = jnp.concatenate([rows_t[:, block_at(first)], rows_t[:, block_at(second)]], axis=1)
        return jnp.concatenate([pair, ones], axis=0)

    fetches[0].wait()
    pl.semaphore_wait(barrier, greeted)
    for k in range(1, Q):
        gather_hi(k).start()
    for k in range(1, Q):
        gather_lo(0, k).start()

    for f in fetches[1:]:
        f.wait()
    for k in range(NB):
        turn(tgt_ref[pl.ds(k * B, B), :], tgt_t, tgt_norm, k)
    for half in range(2):
        put_bias(tgt_bias, tgt_norm[pl.ds(half * HALF, HALF), :] * (-LOG2E / (EPS * SCALE)), half)

    def take(at):
        turn(codes[block_at(at), :], src_t, src_norm, at)

    def first_pair(first, second):
        total = lse_tile(tgt_ref, tgt_bias, under(src_t, first, second))
        vec[0, first // 8, pl.ds(first % 8, 1), :] = total[:, :B]
        vec[0, second // 8, pl.ds(second % 8, 1), :] = total[:, B:]

    for d in range(1, Q):
        gather_hi(d).wait_recv()
        for k in range(1, Q):
            gather_lo(d, k).start()

    @pl.when(is_edge)
    def _():
        signal_all(here_sem.at[0], [across])

    def first_group(d, carry):
        hi = (t_hi - d + Q) % Q
        at = [hi * Q + (t_lo - k + Q) % Q for k in range(Q)]
        take(at[0])
        gather_lo(d, 1).wait_recv()
        take(at[1])
        first_pair(at[0], at[1])
        gather_lo(d, 2).wait_recv()
        take(at[2])
        gather_lo(d, 3).wait_recv()
        take(at[3])
        first_pair(at[2], at[3])

        @pl.when(is_edge & (d == 2))
        def _():
            pl.semaphore_wait(here_sem.at[0], 1)
            signal_all(here_sem.at[1], near_src)

        return carry

    lax.fori_loop(0, Q, first_group, 0)

    def message(e, h, k):
        odd = e % 2
        peer = ((src_me + odd * k) % NB, (tgt_me + (1 - odd) * k) % NB)
        mine = odd * src_me + (1 - odd) * tgt_me
        return copy(vec.at[e, h], inbox.at[e, h, mine], e_send.at[e, h], e_recv.at[e, h], peer)

    def send_half(e, h):
        for k in range(1, NB):
            message(e, h, k).start()
        inbox[e, h, (e % 2) * src_me + (1 - e % 2) * tgt_me] = vec[e, h]

    def all_bytes(e, h, sem):
        others = inbox.at[e, h, pl.ds(0, NB - 1)]
        return pltpu.make_async_copy(others, others, sem.at[e, h])

    def receive(e, h):
        all_bytes(e, h, e_recv).wait()
        pieces = [inbox[e, h, k] for k in range(NB)]
        top = functools.reduce(jnp.maximum, pieces)
        level = top + jnp.log2(functools.reduce(jnp.add, [jnp.exp2(p - top) for p in pieces]))
        side = e % 2
        here = pl.ds(pl.multiple_of(h * HALF, HALF), HALF)
        log = logmass[side, here, :] * LOG2E - level
        put_bias(bias.at[side], log * (1.0 / SCALE), h)
        dual[side, here, :] = log * (EPS / LOG2E) + norm[side, here, :]

    half_rows = pl.ds(pl.multiple_of(src_me % 2 * (N // 2), N // 2), N // 2)

    def spread(k):
        return copy(rows.at[1, half_rows, :], rows.at[1 + k, half_rows, :], x_send.at[k - 1], x_recv.at[k - 1], lo_peer("tgt", k))

    def hand_over(k):
        there = rows.at[1 + k, half_rows, :]
        return copy(there, there, f_send.at[k - 1], f_recv.at[k - 1], {"src": src_me + 1 - 2 * (src_me % 2)})

    def whole_pass(e, carry):
        side = (e - 1) % 2
        late = jnp.minimum(e - 1, 1)
        run_high[...] = jnp.full((8, N), LOW, F32)
        run_total[...] = jnp.zeros((8, N), F32)

        def quarter(s, carry):
            slow, fast = s // 2, s % 2
            h = late * fast + (1 - late) * slow
            m = late * slow + (1 - late) * fast

            @pl.when(s == 0)
            def _():
                receive(e - 1, 0)

            @pl.when(s == 2 * late)
            def _():
                receive(e - 1, 1)

            @pl.when((s == 0) & (e == 1) & ~is_edge)
            def _():
                pl.semaphore_wait(here_sem.at[2], 1)

            @pl.when((s == 0) & (e == 1))
            def _():
                for k in range(1, Q):
                    spread(k).start()

            def body(k, carry):
                at = h * (HALF // 2) + k
                here = pl.ds(pl.multiple_of(at * 2 * B, 2 * B), 2 * B)
                rhs = under(rows_t.at[1 - side], 2 * at, 2 * at + 1)
                run_high[:, here], run_total[:, here] = lse_chunks(
                    rows.at[side], bias.at[side], rhs, m * HALF, HALF, run_high[:, here], run_total[:, here]
                )
                return carry

            lax.fori_loop(0, HALF // 2, body, 0, unroll=UNROLL)

            @pl.when(m == 1)
            def _():
                here = pl.ds(pl.multiple_of(h * (N // 2), N // 2), N // 2)
                out = lse_end(run_high[:, here], run_total[:, here])
                for k in range(HALF):
                    vec[e, h, pl.ds(k, 1), :] = out[:, k * B : (k + 1) * B]
                send_half(e, h)

            return carry

        lax.fori_loop(0, 4, quarter, 0)

        @pl.when(e == 2)
        def _():
            for k in range(1, Q):
                spread(k).wait_recv()
                hand_over(k).start()

        return carry

    send_half(0, 0)
    send_half(0, 1)

    @pl.when(is_edge)
    def _():
        pl.semaphore_wait(here_sem.at[1], len(near_src))
        signal_all(here_sem.at[2], hi_peers)

    lax.fori_loop(1, 4, whole_pass, 0)
    for k in range(1, Q):
        hand_over(k).wait_recv()

    def turn_far(j, carry):
        for k in range(NB):
            rows_t[j, :, pl.ds(k * B, B)] = rows[j, pl.ds(k * B, B), :].astype(F32).T.astype(BF)
        return carry

    lax.fori_loop(2, 2 + Q - 1, turn_far, 0)
    receive(3, 0)
    receive(3, 1)
    sd_ref[...] = dual[0]
    td_ref[...] = dual[1]

    def send_bias(k):
        return copy(far_bias.at[0], far_bias.at[k], b_send.at[k - 1], b_recv.at[k - 1], lo_peer("tgt", k))

    far_bias[0] = (dual[1] - tgt_norm[...]) * (LOG2E / (EPS * SCALE))
    for k in range(1, Q):
        send_bias(k).start()

    near = (t_hi, t_hi + 1 - 2 * (t_hi % 2), (t_hi + 2) % Q, Q - 1 - t_hi)

    def blocks_of(tile):
        first = tile * near[1] + (1 - tile) * near[2]
        second = tile * near[0] + (1 - tile) * near[3]
        return under(src_t, first * Q + t_lo, second * Q + t_lo)

    high[...] = jnp.full((2, 8, 2 * B), LOW, F32)
    mass[...] = jnp.zeros((2, 8, 2 * B), F32)
    moment[...] = jnp.zeros((2, B, 2 * B), F32)

    def add_moments(tile, j):
        top, weight, total = moment_step(
            rows.at[j], rows_t.at[j], bias.at[j], blocks_of(tile), high[tile, pl.ds(0, 1), :], mass[tile], moment[tile]
        )
        high[tile] = jnp.broadcast_to(top, (8, 2 * B))
        mass[tile] = weight
        moment[tile] = total

    def own_moments(tile, carry):
        add_moments(tile, 1)
        return carry

    lax.fori_loop(0, 2, own_moments, 0)
    for k in range(1, Q):
        send_bias(k).wait_recv()
        for half in range(2):
            put_bias(bias.at[1 + k], far_bias[k, pl.ds(half * HALF, HALF), :], half)

    def send_part(r):
        return copy(part.at[r], got.at[r - 1], r_send.at[r - 1], r_recv.at[r - 1], {"tgt": near[r] * Q + t_lo})

    def far_moments(tile, carry):
        def step(j, carry):
            add_moments(tile, j)
            return carry

        lax.fori_loop(2, 2 + Q - 1, step, 0)
        weight = jnp.sum(mass[tile], axis=0, keepdims=True)
        mean = moment[tile] / weight
        level = high[tile] * SCALE + jnp.log2(weight)
        for r, cut in ((2 - tile, pl.ds(0, B)), (3 - 3 * tile, pl.ds(B, B))):
            at = slice(cut.start, cut.start + B)
            part[r, pl.ds(0, B), :] = mean[:, at]
            part[r, pl.ds(B, 8), :] = level[:, at]

        @pl.when(tile == 0)
        def _():
            send_part(2).start()
            send_part(3).start()

        return carry

    lax.fori_loop(0, 2, far_moments, 0)
    send_part(1).start()

    def join(pieces):
        levels = [p[pl.ds(B, 8), :] for p in pieces]
        top = functools.reduce(jnp.maximum, levels)
        scaled = [jnp.exp2(v - top) for v in levels]
        total = functools.reduce(jnp.add, scaled)
        out = None
        for p, v in zip(pieces, scaled):
            term = p[pl.ds(0, B), :] * (v / total)[:1, :]
            out = term if out is None else out + term
        return out

    for r in range(1, Q):
        send_part(r).wait_recv()
    map_ref[...] = join([part.at[0]] + [got.at[j] for j in range(Q - 1)]).T

    for k in range(1, Q):
        gather_hi(k).wait_send()
        spread(k).wait_send()
        hand_over(k).wait_send()
        send_bias(k).wait_send()
        send_part(k).wait_send()
        for d in range(Q):
            gather_lo(d, k).wait_send()
    for e in range(4):
        for h in range(2):
            all_bytes(e, h, e_send).wait()


def hand_on(mapped, src_dual, tgt_dual, mapped_out, src_out, tgt_out):
    mapped_out[...] = mapped[...]
    src_out[...] = src_dual[...]
    tgt_out[...] = tgt_dual[...]


def shards(sources, targets, src_logmass, tgt_logmass):
    vmem = pl.BlockSpec(memory_space=pltpu.VMEM)
    dma = pltpu.SemaphoreType.DMA
    results = (
        jax.ShapeDtypeStruct((B, D), F32),
        jax.ShapeDtypeStruct((NB, B), F32),
        jax.ShapeDtypeStruct((NB, B), F32),
    )
    found = pl.pallas_call(
        kernel,
        out_shape=results,
        in_specs=[pl.BlockSpec(memory_space=pltpu.HBM)] * 4,
        out_specs=(vmem, vmem, vmem),
        scratch_shapes=[
            pltpu.VMEM((1 + Q, N, D), BF),
            pltpu.VMEM((1 + Q, D, N), BF),
            pltpu.VMEM((1 + Q, N, B), BF),
            pltpu.VMEM((FILL, NB, B), F32),
            pltpu.VMEM((2, NB, B), F32),
            pltpu.VMEM((2, NB, B), F32),
            pltpu.VMEM((4, 2, NB // 2, B), F32),
            pltpu.VMEM((4, 2, NB, NB // 2, B), F32),
            pltpu.VMEM((8, N), F32),
            pltpu.VMEM((8, N), F32),
            pltpu.VMEM((2, B, 2 * B), F32),
            pltpu.VMEM((2, 8, 2 * B), F32),
            pltpu.VMEM((2, 8, 2 * B), F32),
            pltpu.VMEM((Q, NB, B), F32),
            pltpu.VMEM((Q, B + 8, D), F32),
            pltpu.VMEM((Q - 1, B + 8, D), F32),
            dma((4,)), pltpu.SemaphoreType.REGULAR((3,)),
            dma((Q - 1,)), dma((Q - 1,)), dma((Q, Q - 1)), dma((Q, Q - 1)),
            dma((4, 2)), dma((4, 2)),
            *[dma((Q - 1,))] * 8,
        ],
        compiler_params=pltpu.CompilerParams(
            collective_id=0, has_side_effects=True, vmem_limit_bytes=64 * 1024 * 1024
        ),
    )(sources, targets, src_logmass.reshape(NB, B), tgt_logmass.reshape(NB, B))
    mapped, src_dual, tgt_dual = pl.pallas_call(
        hand_on,
        out_shape=results,
        in_specs=[vmem] * 3,
        out_specs=(vmem,) * 3,
    )(*found)
    return mapped, src_dual.reshape(N), tgt_dual.reshape(N)


def solution(mesh):
    return jax.shard_map(
        shards,
        mesh=mesh,
        in_specs=(P(("src", "tgt"), None), P("tgt", None), P("src"), P("tgt")),
        out_specs=(P(("src", "tgt"), None), P("src"), P("tgt")),
        check_vma=False,
    )
```

```python
import functools
import math

import jax
import jax.numpy as jnp
from jax import lax
from jax.experimental import pallas as pl
from jax.experimental.pallas import tpu as pltpu
from jax.sharding import PartitionSpec as P

MESH = pl.DeviceIdType.MESH
EPS = 0.03125
LOG2E = math.log2(math.e)
B = 128
NB = 16
N = B * NB
D = 128
Q = 4
SCALE = LOG2E / (D * EPS)
BF = jnp.bfloat16
F32 = jnp.float32


FILL = 6760
GROUP = 16


def fold(x, op):
    x = op(x.reshape(x.shape[0] // GROUP, GROUP, x.shape[1]), axis=0)
    half = GROUP // 2
    return jnp.maximum(x[:half], x[half:]) if op is jnp.max else x[:half] + x[half:]


def lse_chunks(rows, bias, rhs, first, count, high, total):
    for q in range(count):
        at = pl.ds(pl.multiple_of((first + q) * B, B), B)
        u = jnp.dot(jnp.concatenate([rows[at, :], bias[at, :]], axis=1), rhs, preferred_element_type=F32)
        new = jnp.maximum(high, fold(u, jnp.max))
        part = jnp.exp2((u.reshape(B // 8, 8, u.shape[1]) - new[None]) * SCALE).reshape(u.shape)
        total = total * jnp.exp2((high - new) * SCALE) + fold(part, jnp.sum)
        high = new
    return high, total


def lse_end(high, total):
    y = high * SCALE + jnp.log2(total)
    top = jnp.max(y, axis=0, keepdims=True)
    return top + jnp.log2(jnp.sum(jnp.exp2(y - top), axis=0, keepdims=True))


def lse_tile(rows, bias, rhs):
    start = jnp.full((8, rhs.shape[1]), LOW, F32), jnp.zeros((8, rhs.shape[1]), F32)
    return lse_end(*lse_chunks(rows, bias, rhs, 0, NB, *start))


LOW = -1e30
HALF = NB // 2
CHUNK = 256
UNROLL = 4


def moment_step(rows, rows_t, bias, rhs, high, mass, total):
    for q in range(N // CHUNK):
        at = pl.ds(q * CHUNK, CHUNK)
        u = jnp.dot(jnp.concatenate([rows[at, :], bias[at, :]], axis=1), rhs, preferred_element_type=F32)
        new = jnp.maximum(high, jnp.max(fold(u, jnp.max), axis=0, keepdims=True))
        w = jnp.exp2((u - new) * SCALE)
        w_hi = w.astype(BF)
        w_lo = (w - w_hi.astype(F32)).astype(BF)
        lhs = rows_t[:, at]
        ratio = jnp.exp2((high - new) * SCALE)
        mass = mass * ratio + fold(w, jnp.sum)
        part = jnp.dot(lhs, w_hi, preferred_element_type=F32) + jnp.dot(lhs, w_lo, preferred_element_type=F32)
        total = total * ratio + part
        high = new
    return high, mass, total


def kernel(
    src_hbm, tgt_hbm, slm_hbm, tlm_hbm, map_ref, sd_ref, td_ref,
    rows, rows_t, bias, logmass, norm, dual, vec, inbox,
    run_high, run_total, moment, mass, high, far_bias, part, got, in_sem, here_sem,
    g_hi_send, g_hi_recv, g_lo_send, g_lo_recv,
    e_send, e_recv, x_send, x_recv, f_send, f_recv, b_send, b_recv, r_send, r_recv,
):
    src_me = lax.axis_index("src")
    tgt_me = lax.axis_index("tgt")
    s_hi, s_lo = src_me // Q, src_me % Q
    t_hi, t_lo = tgt_me // Q, tgt_me % Q

    def lo_peer(axis, k):
        hi, lo = (s_hi, s_lo) if axis == "src" else (t_hi, t_lo)
        return {axis: hi * Q + (lo + k) % Q}

    def hi_peer(axis, k):
        hi, lo = (s_hi, s_lo) if axis == "src" else (t_hi, t_lo)
        return {axis: ((hi + k) % Q) * Q + lo}

    codes, src_t, src_norm = rows.at[0], rows_t.at[0], norm.at[0]
    tgt_ref, tgt_t, tgt_norm, tgt_bias = rows.at[1], rows_t.at[1], norm.at[1], bias.at[1]

    def block_at(k):
        return pl.ds(pl.multiple_of(k * B, B), B)

    fetches = [
        pltpu.make_async_copy(src, dst, in_sem.at[i])
        for i, (src, dst) in enumerate((
            (src_hbm, codes.at[block_at(tgt_me), :]), (tgt_hbm, tgt_ref), (slm_hbm, logmass.at[0]), (tlm_hbm, logmass.at[1]),
        ))
    ]
    for f in fetches:
        f.start()

    barrier = pltpu.get_barrier_semaphore()
    side, core = s_lo // 2, s_lo % 2
    is_edge = t_hi == (Q - 1) * (1 - side)
    near_src = [
        {"src": ((s_hi + k) % Q) * Q + side * 2 + (core + c) % 2} for k in range(Q) for c in range(2) if k or c
    ]
    across = (s_hi * Q + (1 - side) * 2 + core, (Q - 1 - t_hi) * Q + t_lo)
    hi_peers = [hi_peer("tgt", k) for k in range(1, Q)]

    def signal_all(sem, peers):
        for peer in peers:
            pl.semaphore_signal(sem, 1, device_id=peer, device_id_type=MESH)

    signal_all(barrier, hi_peers + [lo_peer("tgt", k) for k in range(1, Q)] + near_src)

    @pl.when(is_edge)
    def _():
        signal_all(barrier, [across])

    greeted = 2 * (Q - 1) + len(near_src) + 1 - jnp.minimum(jnp.abs(t_hi - (Q - 1) * (1 - side)), 1)

    def copy(src, dst, send, recv, peer):
        return pltpu.make_async_remote_copy(
            src_ref=src, dst_ref=dst, send_sem=send, recv_sem=recv, device_id=peer, device_id_type=MESH
        )

    def gather_hi(k):
        own = codes.at[block_at(tgt_me), :]
        return copy(own, own, g_hi_send.at[k - 1], g_hi_recv.at[k - 1], hi_peer("tgt", k))

    def gather_lo(d, k):
        block = ((t_hi - d + Q) % Q) * Q + t_lo
        rows = codes.at[block_at(block), :]
        return copy(rows, rows, g_lo_send.at[d, k - 1], g_lo_recv.at[d, k - 1], lo_peer("tgt", k))

    lane = lax.broadcasted_iota(jnp.int32, (B, B), 1)
    ones = jnp.ones((D, 2 * B), BF)

    def put_bias(out, values, half):
        hi = values.astype(BF).astype(F32)
        rest = values - hi
        mid = rest.astype(BF).astype(F32)
        low = rest - mid
        turned = jnp.concatenate([hi, mid, low, jnp.zeros((B - 3 * HALF, B), F32)], axis=0).T
        for k in range(HALF):
            out[block_at(half * HALF + k), :] = jnp.where(lane % HALF == k, turned, 0.0).astype(BF)

    def turn(rows, rows_t, norm, at):
        turned = rows.astype(F32).T
        rows_t[:, block_at(at)] = turned.astype(BF)
        norm[pl.ds(at, 1), :] = jnp.sum(turned * turned, axis=0, keepdims=True) * (0.5 / D)

    def under(rows_t, first, second):
        pair = jnp.concatenate([rows_t[:, block_at(first)], rows_t[:, block_at(second)]], axis=1)
        return jnp.concatenate([pair, ones], axis=0)

    fetches[0].wait()
    pl.semaphore_wait(barrier, greeted)
    for k in range(1, Q):
        gather_hi(k).start()
    for k in range(1, Q):
        gather_lo(0, k).start()

    for f in fetches[1:]:
        f.wait()
    for k in range(NB):
        turn(tgt_ref[pl.ds(k * B, B), :], tgt_t, tgt_norm, k)
    for half in range(2):
        put_bias(tgt_bias, tgt_norm[pl.ds(half * HALF, HALF), :] * (-LOG2E / (EPS * SCALE)), half)

    def take(at):
        turn(codes[block_at(at), :], src_t, src_norm, at)

    def first_pair(first, second):
        total = lse_tile(tgt_ref, tgt_bias, under(src_t, first, second))
        vec[0, first // 8, pl.ds(first % 8, 1), :] = total[:, :B]
        vec[0, second // 8, pl.ds(second % 8, 1), :] = total[:, B:]

    for d in range(1, Q):
        gather_hi(d).wait_recv()
        for k in range(1, Q):
            gather_lo(d, k).start()

    @pl.when(is_edge)
    def _():
        signal_all(here_sem.at[0], [across])

    def first_group(d, carry):
        hi = (t_hi - d + Q) % Q
        at = [hi * Q + (t_lo - k + Q) % Q for k in range(Q)]
        take(at[0])
        gather_lo(d, 1).wait_recv()
        take(at[1])
        first_pair(at[0], at[1])
        gather_lo(d, 2).wait_recv()
        take(at[2])
        gather_lo(d, 3).wait_recv()
        take(at[3])
        first_pair(at[2], at[3])

        @pl.when(is_edge & (d == 2))
        def _():
            pl.semaphore_wait(here_sem.at[0], 1)
            signal_all(here_sem.at[1], near_src)

        return carry

    lax.fori_loop(0, Q, first_group, 0)

    def message(e, h, k):
        odd = e % 2
        peer = ((src_me + odd * k) % NB, (tgt_me + (1 - odd) * k) % NB)
        mine = odd * src_me + (1 - odd) * tgt_me
        return copy(vec.at[e, h], inbox.at[e, h, mine], e_send.at[e, h], e_recv.at[e, h], peer)

    def send_half(e, h):
        for k in range(1, NB):
            message(e, h, k).start()
        inbox[e, h, (e % 2) * src_me + (1 - e % 2) * tgt_me] = vec[e, h]

    def all_bytes(e, h, sem):
        others = inbox.at[e, h, pl.ds(0, NB - 1)]
        return pltpu.make_async_copy(others, others, sem.at[e, h])

    def receive(e, h):
        all_bytes(e, h, e_recv).wait()
        pieces = [inbox[e, h, k] for k in range(NB)]
        top = functools.reduce(jnp.maximum, pieces)
        level = top + jnp.log2(functools.reduce(jnp.add, [jnp.exp2(p - top) for p in pieces]))
        side = e % 2
        here = pl.ds(pl.multiple_of(h * HALF, HALF), HALF)
        log = logmass[side, here, :] * LOG2E - level
        put_bias(bias.at[side], log * (1.0 / SCALE), h)
        dual[side, here, :] = log * (EPS / LOG2E) + norm[side, here, :]

    half_rows = pl.ds(pl.multiple_of(src_me % 2 * (N // 2), N // 2), N // 2)

    def spread(k):
        return copy(rows.at[1, half_rows, :], rows.at[1 + k, half_rows, :], x_send.at[k - 1], x_recv.at[k - 1], lo_peer("tgt", k))

    def hand_over(k):
        there = rows.at[1 + k, half_rows, :]
        return copy(there, there, f_send.at[k - 1], f_recv.at[k - 1], {"src": src_me + 1 - 2 * (src_me % 2)})

    def whole_pass(e, carry):
        side = (e - 1) % 2
        late = jnp.minimum(e - 1, 1)
        run_high[...] = jnp.full((8, N), LOW, F32)
        run_total[...] = jnp.zeros((8, N), F32)

        def quarter(s, carry):
            slow, fast = s // 2, s % 2
            h = late * fast + (1 - late) * slow
            m = late * slow + (1 - late) * fast

            @pl.when(s == 0)
            def _():
                receive(e - 1, 0)

            @pl.when(s == 2 * late)
            def _():
                receive(e - 1, 1)

            @pl.when((s == 0) & (e == 1) & ~is_edge)
            def _():
                pl.semaphore_wait(here_sem.at[2], 1)

            @pl.when((s == 0) & (e == 1))
            def _():
                for k in range(1, Q):
                    spread(k).start()

            def body(k, carry):
                at = h * (HALF // 2) + k
                here = pl.ds(pl.multiple_of(at * 2 * B, 2 * B), 2 * B)
                rhs = under(rows_t.at[1 - side], 2 * at, 2 * at + 1)
                run_high[:, here], run_total[:, here] = lse_chunks(
                    rows.at[side], bias.at[side], rhs, m * HALF, HALF, run_high[:, here], run_total[:, here]
                )
                return carry

            lax.fori_loop(0, HALF // 2, body, 0, unroll=UNROLL)

            @pl.when(m == 1)
            def _():
                here = pl.ds(pl.multiple_of(h * (N // 2), N // 2), N // 2)
                out = lse_end(run_high[:, here], run_total[:, here])
                for k in range(HALF):
                    vec[e, h, pl.ds(k, 1), :] = out[:, k * B : (k + 1) * B]
                send_half(e, h)

            return carry

        lax.fori_loop(0, 4, quarter, 0)

        @pl.when(e == 2)
        def _():
            for k in range(1, Q):
                spread(k).wait_recv()
                hand_over(k).start()

        return carry

    send_half(0, 0)
    send_half(0, 1)

    @pl.when(is_edge)
    def _():
        pl.semaphore_wait(here_sem.at[1], len(near_src))
        signal_all(here_sem.at[2], hi_peers)

    lax.fori_loop(1, 4, whole_pass, 0)
    for k in range(1, Q):
        hand_over(k).wait_recv()

    def turn_far(j, carry):
        for k in range(NB):
            rows_t[j, :, pl.ds(k * B, B)] = rows[j, pl.ds(k * B, B), :].astype(F32).T.astype(BF)
        return carry

    lax.fori_loop(2, 2 + Q - 1, turn_far, 0)
    receive(3, 0)
    receive(3, 1)
    sd_ref[...] = dual[0]
    td_ref[...] = dual[1]

    def send_bias(k):
        return copy(far_bias.at[0], far_bias.at[k], b_send.at[k - 1], b_recv.at[k - 1], lo_peer("tgt", k))

    far_bias[0] = (dual[1] - tgt_norm[...]) * (LOG2E / (EPS * SCALE))
    for k in range(1, Q):
        send_bias(k).start()

    near = (t_hi, t_hi + 1 - 2 * (t_hi % 2), (t_hi + 2) % Q, Q - 1 - t_hi)

    def blocks_of(tile):
        first = tile * near[1] + (1 - tile) * near[2]
        second = tile * near[0] + (1 - tile) * near[3]
        return under(src_t, first * Q + t_lo, second * Q + t_lo)

    high[...] = jnp.full((2, 8, 2 * B), LOW, F32)
    mass[...] = jnp.zeros((2, 8, 2 * B), F32)
    moment[...] = jnp.zeros((2, B, 2 * B), F32)

    def add_moments(tile, j):
        top, weight, total = moment_step(
            rows.at[j], rows_t.at[j], bias.at[j], blocks_of(tile), high[tile, pl.ds(0, 1), :], mass[tile], moment[tile]
        )
        high[tile] = jnp.broadcast_to(top, (8, 2 * B))
        mass[tile] = weight
        moment[tile] = total

    def own_moments(tile, carry):
        add_moments(tile, 1)
        return carry

    lax.fori_loop(0, 2, own_moments, 0)

    def take_bias(k):
        send_bias(k).wait_recv()
        for half in range(2):
            put_bias(bias.at[1 + k], far_bias[k, pl.ds(half * HALF, HALF), :], half)

    take_bias(1)
    take_bias(3)

    def send_part(r):
        return copy(part.at[r], got.at[r - 1], r_send.at[r - 1], r_recv.at[r - 1], {"tgt": near[r] * Q + t_lo})

    def far_moments(tile, carry):
        def step(j, carry):
            add_moments(tile, 2 + 2 * j)
            return carry

        lax.fori_loop(0, 2, step, 0)

        @pl.when(tile == 0)
        def _():
            take_bias(2)

        add_moments(tile, 3)
        weight = jnp.sum(mass[tile], axis=0, keepdims=True)
        mean = moment[tile] / weight
        level = high[tile] * SCALE + jnp.log2(weight)
        for r, cut in ((2 - tile, pl.ds(0, B)), (3 - 3 * tile, pl.ds(B, B))):
            at = slice(cut.start, cut.start + B)
            part[r, pl.ds(0, B), :] = mean[:, at]
            part[r, pl.ds(B, 8), :] = level[:, at]

        @pl.when(tile == 0)
        def _():
            send_part(2).start()
            send_part(3).start()

        return carry

    lax.fori_loop(0, 2, far_moments, 0)
    send_part(1).start()

    def join(pieces):
        levels = [p[pl.ds(B, 8), :] for p in pieces]
        top = functools.reduce(jnp.maximum, levels)
        scaled = [jnp.exp2(v - top) for v in levels]
        total = functools.reduce(jnp.add, scaled)
        out = None
        for p, v in zip(pieces, scaled):
            term = p[pl.ds(0, B), :] * (v / total)[:1, :]
            out = term if out is None else out + term
        return out

    for r in range(1, Q):
        send_part(r).wait_recv()
    map_ref[...] = join([part.at[0]] + [got.at[j] for j in range(Q - 1)]).T

    for k in range(1, Q):
        gather_hi(k).wait_send()
        spread(k).wait_send()
        hand_over(k).wait_send()
        send_bias(k).wait_send()
        send_part(k).wait_send()
        for d in range(Q):
            gather_lo(d, k).wait_send()
    for e in range(4):
        for h in range(2):
            all_bytes(e, h, e_send).wait()


def hand_on(mapped, src_dual, tgt_dual, mapped_out, src_out, tgt_out):
    mapped_out[...] = mapped[...]
    src_out[...] = src_dual[...]
    tgt_out[...] = tgt_dual[...]


def shards(sources, targets, src_logmass, tgt_logmass):
    vmem = pl.BlockSpec(memory_space=pltpu.VMEM)
    dma = pltpu.SemaphoreType.DMA
    results = (
        jax.ShapeDtypeStruct((B, D), F32),
        jax.ShapeDtypeStruct((NB, B), F32),
        jax.ShapeDtypeStruct((NB, B), F32),
    )
    found = pl.pallas_call(
        kernel,
        out_shape=results,
        in_specs=[pl.BlockSpec(memory_space=pltpu.HBM)] * 4,
        out_specs=(vmem, vmem, vmem),
        scratch_shapes=[
            pltpu.VMEM((1 + Q, N, D), BF),
            pltpu.VMEM((1 + Q, D, N), BF),
            pltpu.VMEM((1 + Q, N, B), BF),
            pltpu.VMEM((FILL, NB, B), F32),
            pltpu.VMEM((2, NB, B), F32),
            pltpu.VMEM((2, NB, B), F32),
            pltpu.VMEM((4, 2, NB // 2, B), F32),
            pltpu.VMEM((4, 2, NB, NB // 2, B), F32),
            pltpu.VMEM((8, N), F32),
            pltpu.VMEM((8, N), F32),
            pltpu.VMEM((2, B, 2 * B), F32),
            pltpu.VMEM((2, 8, 2 * B), F32),
            pltpu.VMEM((2, 8, 2 * B), F32),
            pltpu.VMEM((Q, NB, B), F32),
            pltpu.VMEM((Q, B + 8, D), F32),
            pltpu.VMEM((Q - 1, B + 8, D), F32),
            dma((4,)), pltpu.SemaphoreType.REGULAR((3,)),
            dma((Q - 1,)), dma((Q - 1,)), dma((Q, Q - 1)), dma((Q, Q - 1)),
            dma((4, 2)), dma((4, 2)),
            *[dma((Q - 1,))] * 8,
        ],
        compiler_params=pltpu.CompilerParams(
            collective_id=0, has_side_effects=True, vmem_limit_bytes=64 * 1024 * 1024
        ),
    )(sources, targets, src_logmass.reshape(NB, B), tgt_logmass.reshape(NB, B))
    mapped, src_dual, tgt_dual = pl.pallas_call(
        hand_on,
        out_shape=results,
        in_specs=[vmem] * 3,
        out_specs=(vmem,) * 3,
    )(*found)
    return mapped, src_dual.reshape(N), tgt_dual.reshape(N)


def solution(mesh):
    return jax.shard_map(
        shards,
        mesh=mesh,
        in_specs=(P(("src", "tgt"), None), P("tgt", None), P("src"), P("tgt")),
        out_specs=(P(("src", "tgt"), None), P("src"), P("tgt")),
        check_vma=False,
    )
```

```python
import functools
import math

import jax
import jax.numpy as jnp
from jax import lax
from jax.experimental import pallas as pl
from jax.experimental.pallas import tpu as pltpu
from jax.sharding import PartitionSpec as P

MESH = pl.DeviceIdType.MESH
EPS = 0.03125
LOG2E = math.log2(math.e)
B = 128
NB = 16
N = B * NB
D = 128
Q = 4
SCALE = LOG2E / (D * EPS)
BF = jnp.bfloat16
F32 = jnp.float32


FILL = 6760
GROUP = 16


def fold(x, op):
    x = op(x.reshape(x.shape[0] // GROUP, GROUP, x.shape[1]), axis=0)
    half = GROUP // 2
    return jnp.maximum(x[:half], x[half:]) if op is jnp.max else x[:half] + x[half:]


def lse_chunks(rows, bias, rhs, first, count, high, total):
    for q in range(count):
        at = pl.ds(pl.multiple_of((first + q) * B, B), B)
        u = jnp.dot(jnp.concatenate([rows[at, :], bias[at, :]], axis=1), rhs, preferred_element_type=F32)
        new = jnp.maximum(high, fold(u, jnp.max))
        part = jnp.exp2((u.reshape(B // 8, 8, u.shape[1]) - new[None]) * SCALE).reshape(u.shape)
        total = total * jnp.exp2((high - new) * SCALE) + fold(part, jnp.sum)
        high = new
    return high, total


def lse_end(high, total):
    y = high * SCALE + jnp.log2(total)
    top = jnp.max(y, axis=0, keepdims=True)
    return top + jnp.log2(jnp.sum(jnp.exp2(y - top), axis=0, keepdims=True))


def lse_tile(rows, bias, rhs):
    start = jnp.full((8, rhs.shape[1]), LOW, F32), jnp.zeros((8, rhs.shape[1]), F32)
    return lse_end(*lse_chunks(rows, bias, rhs, 0, NB, *start))


LOW = -1e30
HALF = NB // 2
CHUNK = 256
UNROLL = 4


def moment_step(rows, rows_t, bias, rhs, high, mass, total):
    for q in range(N // CHUNK):
        at = pl.ds(q * CHUNK, CHUNK)
        u = jnp.dot(jnp.concatenate([rows[at, :], bias[at, :]], axis=1), rhs, preferred_element_type=F32)
        new = jnp.maximum(high, jnp.max(fold(u, jnp.max), axis=0, keepdims=True))
        w = jnp.exp2((u - new) * SCALE)
        w_hi = w.astype(BF)
        w_lo = (w - w_hi.astype(F32)).astype(BF)
        lhs = rows_t[:, at]
        ratio = jnp.exp2((high - new) * SCALE)
        mass = mass * ratio + fold(w, jnp.sum)
        part = jnp.dot(lhs, w_hi, preferred_element_type=F32) + jnp.dot(lhs, w_lo, preferred_element_type=F32)
        total = total * ratio + part
        high = new
    return high, mass, total


def kernel(
    src_hbm, tgt_hbm, slm_hbm, tlm_hbm, map_ref, sd_ref, td_ref,
    rows, rows_t, bias, logmass, norm, dual, vec, inbox,
    run_high, run_total, moment, mass, high, far_bias, part, got, in_sem, here_sem,
    g_hi_send, g_hi_recv, g_lo_send, g_lo_recv,
    e_send, e_recv, x_send, x_recv, f_send, f_recv, b_send, b_recv, r_send, r_recv,
):
    src_me = lax.axis_index("src")
    tgt_me = lax.axis_index("tgt")
    s_hi, s_lo = src_me // Q, src_me % Q
    t_hi, t_lo = tgt_me // Q, tgt_me % Q

    def lo_peer(axis, k):
        hi, lo = (s_hi, s_lo) if axis == "src" else (t_hi, t_lo)
        return {axis: hi * Q + (lo + k) % Q}

    def hi_peer(axis, k):
        hi, lo = (s_hi, s_lo) if axis == "src" else (t_hi, t_lo)
        return {axis: ((hi + k) % Q) * Q + lo}

    codes, src_t, src_norm = rows.at[0], rows_t.at[0], norm.at[0]
    tgt_ref, tgt_t, tgt_norm, tgt_bias = rows.at[1], rows_t.at[1], norm.at[1], bias.at[1]

    def block_at(k):
        return pl.ds(pl.multiple_of(k * B, B), B)

    fetches = [
        pltpu.make_async_copy(src, dst, in_sem.at[i])
        for i, (src, dst) in enumerate((
            (src_hbm, codes.at[block_at(tgt_me), :]), (tgt_hbm, tgt_ref), (slm_hbm, logmass.at[0]), (tlm_hbm, logmass.at[1]),
        ))
    ]
    for f in fetches:
        f.start()

    barrier = pltpu.get_barrier_semaphore()
    side, core = s_lo // 2, s_lo % 2
    is_edge = t_hi == (Q - 1) * (1 - side)
    near_src = [
        {"src": ((s_hi + k) % Q) * Q + side * 2 + (core + c) % 2} for k in range(Q) for c in range(2) if k or c
    ]
    across = (s_hi * Q + (1 - side) * 2 + core, (Q - 1 - t_hi) * Q + t_lo)
    hi_peers = [hi_peer("tgt", k) for k in range(1, Q)]

    def signal_all(sem, peers):
        for peer in peers:
            pl.semaphore_signal(sem, 1, device_id=peer, device_id_type=MESH)

    signal_all(barrier, hi_peers + [lo_peer("tgt", k) for k in range(1, Q)] + near_src)

    @pl.when(is_edge)
    def _():
        signal_all(barrier, [across])

    greeted = 2 * (Q - 1) + len(near_src) + 1 - jnp.minimum(jnp.abs(t_hi - (Q - 1) * (1 - side)), 1)

    def copy(src, dst, send, recv, peer):
        return pltpu.make_async_remote_copy(
            src_ref=src, dst_ref=dst, send_sem=send, recv_sem=recv, device_id=peer, device_id_type=MESH
        )

    def gather_hi(k):
        own = codes.at[block_at(tgt_me), :]
        return copy(own, own, g_hi_send.at[k - 1], g_hi_recv.at[k - 1], hi_peer("tgt", k))

    def gather_lo(d, k):
        block = ((t_hi - d + Q) % Q) * Q + t_lo
        rows = codes.at[block_at(block), :]
        return copy(rows, rows, g_lo_send.at[d, k - 1], g_lo_recv.at[d, k - 1], lo_peer("tgt", k))

    lane = lax.broadcasted_iota(jnp.int32, (B, B), 1)
    ones = jnp.ones((D, 2 * B), BF)

    def put_bias(out, values, half):
        hi = values.astype(BF).astype(F32)
        rest = values - hi
        mid = rest.astype(BF).astype(F32)
        low = rest - mid
        turned = jnp.concatenate([hi, mid, low, jnp.zeros((B - 3 * HALF, B), F32)], axis=0).T
        for k in range(HALF):
            out[block_at(half * HALF + k), :] = jnp.where(lane % HALF == k, turned, 0.0).astype(BF)

    def turn(rows, rows_t, norm, at):
        turned = rows.astype(F32).T
        rows_t[:, block_at(at)] = turned.astype(BF)
        norm[pl.ds(at, 1), :] = jnp.sum(turned * turned, axis=0, keepdims=True) * (0.5 / D)

    def under(rows_t, first, second):
        pair = jnp.concatenate([rows_t[:, block_at(first)], rows_t[:, block_at(second)]], axis=1)
        return jnp.concatenate([pair, ones], axis=0)

    fetches[0].wait()
    pl.semaphore_wait(barrier, greeted)
    for k in range(1, Q):
        gather_hi(k).start()
    for k in range(1, Q):
        gather_lo(0, k).start()

    for f in fetches[1:]:
        f.wait()
    for k in range(NB):
        turn(tgt_ref[pl.ds(k * B, B), :], tgt_t, tgt_norm, k)
    for half in range(2):
        put_bias(tgt_bias, tgt_norm[pl.ds(half * HALF, HALF), :] * (-LOG2E / (EPS * SCALE)), half)

    def take(at):
        turn(codes[block_at(at), :], src_t, src_norm, at)

    def first_pair(first, second):
        total = lse_tile(tgt_ref, tgt_bias, under(src_t, first, second))
        vec[0, first // 8, pl.ds(first % 8, 1), :] = total[:, :B]
        vec[0, second // 8, pl.ds(second % 8, 1), :] = total[:, B:]

    for d in range(1, Q):
        gather_hi(d).wait_recv()
        for k in range(1, Q):
            gather_lo(d, k).start()

    @pl.when(is_edge)
    def _():
        signal_all(here_sem.at[0], [across])

    def first_group(d, carry):
        hi = (t_hi - d + Q) % Q
        at = [hi * Q + (t_lo - k + Q) % Q for k in range(Q)]
        take(at[0])
        gather_lo(d, 1).wait_recv()
        take(at[1])
        first_pair(at[0], at[1])
        gather_lo(d, 3).wait_recv()
        take(at[3])
        gather_lo(d, 2).wait_recv()
        take(at[2])
        first_pair(at[3], at[2])

        @pl.when(is_edge & (d == 2))
        def _():
            pl.semaphore_wait(here_sem.at[0], 1)
            signal_all(here_sem.at[1], near_src)

        return carry

    lax.fori_loop(0, Q, first_group, 0)

    def message(e, h, k):
        odd = e % 2
        peer = ((src_me + odd * k) % NB, (tgt_me + (1 - odd) * k) % NB)
        mine = odd * src_me + (1 - odd) * tgt_me
        return copy(vec.at[e, h], inbox.at[e, h, mine], e_send.at[e, h], e_recv.at[e, h], peer)

    def send_half(e, h):
        for k in range(1, NB):
            message(e, h, k).start()
        inbox[e, h, (e % 2) * src_me + (1 - e % 2) * tgt_me] = vec[e, h]

    def all_bytes(e, h, sem):
        others = inbox.at[e, h, pl.ds(0, NB - 1)]
        return pltpu.make_async_copy(others, others, sem.at[e, h])

    def receive(e, h):
        all_bytes(e, h, e_recv).wait()
        pieces = [inbox[e, h, k] for k in range(NB)]
        top = functools.reduce(jnp.maximum, pieces)
        level = top + jnp.log2(functools.reduce(jnp.add, [jnp.exp2(p - top) for p in pieces]))
        side = e % 2
        here = pl.ds(pl.multiple_of(h * HALF, HALF), HALF)
        log = logmass[side, here, :] * LOG2E - level
        put_bias(bias.at[side], log * (1.0 / SCALE), h)
        dual[side, here, :] = log * (EPS / LOG2E) + norm[side, here, :]

    half_rows = pl.ds(pl.multiple_of(src_me % 2 * (N // 2), N // 2), N // 2)

    def spread(k):
        return copy(rows.at[1, half_rows, :], rows.at[1 + k, half_rows, :], x_send.at[k - 1], x_recv.at[k - 1], lo_peer("tgt", k))

    def hand_over(k):
        there = rows.at[1 + k, half_rows, :]
        return copy(there, there, f_send.at[k - 1], f_recv.at[k - 1], {"src": src_me + 1 - 2 * (src_me % 2)})

    def whole_pass(e, carry):
        side = (e - 1) % 2
        late = jnp.minimum(e - 1, 1)
        run_high[...] = jnp.full((8, N), LOW, F32)
        run_total[...] = jnp.zeros((8, N), F32)

        def quarter(s, carry):
            slow, fast = s // 2, s % 2
            h = late * fast + (1 - late) * slow
            m = late * slow + (1 - late) * fast

            @pl.when(s == 0)
            def _():
                receive(e - 1, 0)

            @pl.when(s == 2 * late)
            def _():
                receive(e - 1, 1)

            @pl.when((s == 0) & (e == 1) & ~is_edge)
            def _():
                pl.semaphore_wait(here_sem.at[2], 1)

            @pl.when((s == 0) & (e == 1))
            def _():
                for k in range(1, Q):
                    spread(k).start()

            def body(k, carry):
                at = h * (HALF // 2) + k
                here = pl.ds(pl.multiple_of(at * 2 * B, 2 * B), 2 * B)
                rhs = under(rows_t.at[1 - side], 2 * at, 2 * at + 1)
                run_high[:, here], run_total[:, here] = lse_chunks(
                    rows.at[side], bias.at[side], rhs, m * HALF, HALF, run_high[:, here], run_total[:, here]
                )
                return carry

            lax.fori_loop(0, HALF // 2, body, 0, unroll=UNROLL)

            @pl.when(m == 1)
            def _():
                here = pl.ds(pl.multiple_of(h * (N // 2), N // 2), N // 2)
                out = lse_end(run_high[:, here], run_total[:, here])
                for k in range(HALF):
                    vec[e, h, pl.ds(k, 1), :] = out[:, k * B : (k + 1) * B]
                send_half(e, h)

            return carry

        lax.fori_loop(0, 4, quarter, 0)

        @pl.when(e == 2)
        def _():
            for k in range(1, Q):
                spread(k).wait_recv()
                hand_over(k).start()

        return carry

    send_half(0, 0)
    send_half(0, 1)

    @pl.when(is_edge)
    def _():
        pl.semaphore_wait(here_sem.at[1], len(near_src))
        signal_all(here_sem.at[2], hi_peers)

    lax.fori_loop(1, 4, whole_pass, 0)
    for k in range(1, Q):
        hand_over(k).wait_recv()

    def turn_far(j, carry):
        for k in range(NB):
            rows_t[j, :, pl.ds(k * B, B)] = rows[j, pl.ds(k * B, B), :].astype(F32).T.astype(BF)
        return carry

    lax.fori_loop(2, 2 + Q - 1, turn_far, 0)
    receive(3, 0)
    receive(3, 1)
    sd_ref[...] = dual[0]
    td_ref[...] = dual[1]

    def send_bias(k):
        return copy(far_bias.at[0], far_bias.at[k], b_send.at[k - 1], b_recv.at[k - 1], lo_peer("tgt", k))

    far_bias[0] = (dual[1] - tgt_norm[...]) * (LOG2E / (EPS * SCALE))
    for k in range(1, Q):
        send_bias(k).start()

    near = (t_hi, t_hi + 1 - 2 * (t_hi % 2), (t_hi + 2) % Q, Q - 1 - t_hi)

    def blocks_of(tile):
        first = tile * near[1] + (1 - tile) * near[2]
        second = tile * near[0] + (1 - tile) * near[3]
        return under(src_t, first * Q + t_lo, second * Q + t_lo)

    high[...] = jnp.full((2, 8, 2 * B), LOW, F32)
    mass[...] = jnp.zeros((2, 8, 2 * B), F32)
    moment[...] = jnp.zeros((2, B, 2 * B), F32)

    def add_moments(tile, j):
        top, weight, total = moment_step(
            rows.at[j], rows_t.at[j], bias.at[j], blocks_of(tile), high[tile, pl.ds(0, 1), :], mass[tile], moment[tile]
        )
        high[tile] = jnp.broadcast_to(top, (8, 2 * B))
        mass[tile] = weight
        moment[tile] = total

    def own_moments(tile, carry):
        add_moments(tile, 1)
        return carry

    lax.fori_loop(0, 2, own_moments, 0)

    def take_bias(k):
        send_bias(k).wait_recv()
        for half in range(2):
            put_bias(bias.at[1 + k], far_bias[k, pl.ds(half * HALF, HALF), :], half)

    take_bias(1)
    take_bias(3)

    def send_part(r):
        return copy(part.at[r], got.at[r - 1], r_send.at[r - 1], r_recv.at[r - 1], {"tgt": near[r] * Q + t_lo})

    def far_moments(tile, carry):
        def step(j, carry):
            add_moments(tile, 2 + 2 * j)
            return carry

        lax.fori_loop(0, 2, step, 0)

        @pl.when(tile == 0)
        def _():
            take_bias(2)

        add_moments(tile, 3)
        weight = jnp.sum(mass[tile], axis=0, keepdims=True)
        mean = moment[tile] / weight
        level = high[tile] * SCALE + jnp.log2(weight)
        for r, cut in ((2 - tile, pl.ds(0, B)), (3 - 3 * tile, pl.ds(B, B))):
            at = slice(cut.start, cut.start + B)
            part[r, pl.ds(0, B), :] = mean[:, at]
            part[r, pl.ds(B, 8), :] = level[:, at]

        @pl.when(tile == 0)
        def _():
            send_part(2).start()
            send_part(3).start()

        return carry

    lax.fori_loop(0, 2, far_moments, 0)
    send_part(1).start()

    def join(pieces):
        levels = [p[pl.ds(B, 8), :] for p in pieces]
        top = functools.reduce(jnp.maximum, levels)
        scaled = [jnp.exp2(v - top) for v in levels]
        total = functools.reduce(jnp.add, scaled)
        out = None
        for p, v in zip(pieces, scaled):
            term = p[pl.ds(0, B), :] * (v / total)[:1, :]
            out = term if out is None else out + term
        return out

    for r in range(1, Q):
        send_part(r).wait_recv()
    map_ref[...] = join([part.at[0]] + [got.at[j] for j in range(Q - 1)]).T

    for k in range(1, Q):
        gather_hi(k).wait_send()
        spread(k).wait_send()
        hand_over(k).wait_send()
        send_bias(k).wait_send()
        send_part(k).wait_send()
        for d in range(Q):
            gather_lo(d, k).wait_send()
    for e in range(4):
        for h in range(2):
            all_bytes(e, h, e_send).wait()


def hand_on(mapped, src_dual, tgt_dual, mapped_out, src_out, tgt_out):
    mapped_out[...] = mapped[...]
    src_out[...] = src_dual[...]
    tgt_out[...] = tgt_dual[...]


def shards(sources, targets, src_logmass, tgt_logmass):
    vmem = pl.BlockSpec(memory_space=pltpu.VMEM)
    dma = pltpu.SemaphoreType.DMA
    results = (
        jax.ShapeDtypeStruct((B, D), F32),
        jax.ShapeDtypeStruct((NB, B), F32),
        jax.ShapeDtypeStruct((NB, B), F32),
    )
    found = pl.pallas_call(
        kernel,
        out_shape=results,
        in_specs=[pl.BlockSpec(memory_space=pltpu.HBM)] * 4,
        out_specs=(vmem, vmem, vmem),
        scratch_shapes=[
            pltpu.VMEM((1 + Q, N, D), BF),
            pltpu.VMEM((1 + Q, D, N), BF),
            pltpu.VMEM((1 + Q, N, B), BF),
            pltpu.VMEM((FILL, NB, B), F32),
            pltpu.VMEM((2, NB, B), F32),
            pltpu.VMEM((2, NB, B), F32),
            pltpu.VMEM((4, 2, NB // 2, B), F32),
            pltpu.VMEM((4, 2, NB, NB // 2, B), F32),
            pltpu.VMEM((8, N), F32),
            pltpu.VMEM((8, N), F32),
            pltpu.VMEM((2, B, 2 * B), F32),
            pltpu.VMEM((2, 8, 2 * B), F32),
            pltpu.VMEM((2, 8, 2 * B), F32),
            pltpu.VMEM((Q, NB, B), F32),
            pltpu.VMEM((Q, B + 8, D), F32),
            pltpu.VMEM((Q - 1, B + 8, D), F32),
            dma((4,)), pltpu.SemaphoreType.REGULAR((3,)),
            dma((Q - 1,)), dma((Q - 1,)), dma((Q, Q - 1)), dma((Q, Q - 1)),
            dma((4, 2)), dma((4, 2)),
            *[dma((Q - 1,))] * 8,
        ],
        compiler_params=pltpu.CompilerParams(
            collective_id=0, has_side_effects=True, vmem_limit_bytes=64 * 1024 * 1024
        ),
    )(sources, targets, src_logmass.reshape(NB, B), tgt_logmass.reshape(NB, B))
    mapped, src_dual, tgt_dual = pl.pallas_call(
        hand_on,
        out_shape=results,
        in_specs=[vmem] * 3,
        out_specs=(vmem,) * 3,
    )(*found)
    return mapped, src_dual.reshape(N), tgt_dual.reshape(N)


def solution(mesh):
    return jax.shard_map(
        shards,
        mesh=mesh,
        in_specs=(P(("src", "tgt"), None), P("tgt", None), P("src"), P("tgt")),
        out_specs=(P(("src", "tgt"), None), P("src"), P("tgt")),
        check_vma=False,
    )
```
